512 devices in a mesh: res: 128 (over y_lo, z, x), cx: 4 (over y_hi, core).
Axes of the slice: x: 4, y: 4 (y_hi: 2, y_lo: 2; y = y_hi * 2 + y_lo), z: 16, core: 2. Of those that a mesh axis runs over, the one named last changes fastest.
Arguments:
- homolog_representation: bfloat16 [128, 256, 256], P('cx', 'res'), parts along dimension 0, may hold values from -6 to 6
- pairwise_representation: bfloat16 [1024, 256, 128], P(('cx', 'res')), parts along dimension 0, may hold values from -6 to 6
- pairwise_refreshed_adjoint: bfloat16 [1024, 256, 128], P(('cx', 'res')), parts along dimension 0, may hold values from -6 to 6
- homolog_standard_multiplier: float32 [256], replicated, may hold values from 0.5 to 2
- pairwise_standard_multiplier: float32 [128], replicated, may hold values from 0.5 to 2
- paired_linear_operators: bfloat16 [256, 64], replicated, may hold values from -0.375 to 0.375
- closing_linear_operator: bfloat16 [1024, 128], replicated, may hold values from -0.75 to 0.75
- widening_transition_weights: bfloat16 [128, 512], replicated, may hold values from -0.5 to 0.5
- narrowing_transition_weights: bfloat16 [512, 128], replicated, may hold values from -0.25 to 0.25
Outputs:
- pair_output: bfloat16 [1024, 256, 128], P(('cx', 'res')), parts along dimension 0
- pair_gradient: bfloat16 [1024, 256, 128], P(('cx', 'res')), parts along dimension 0
- homolog_array_slope: bfloat16 [128, 256, 256], P('cx', 'res'), parts along dimension 0
- grad_out: float32 [4096, 128], P('cx'), parts along dimension 0
- projection_weight_gradient: float32 [1024, 64], P('cx'), parts along dimension 0
- grad_up: float32 [512, 512], P('cx'), parts along dimension 0
- grad_down: float32 [2048, 128], P('cx'), parts along dimension 0
The draws below stay inside these ranges and needn't reach their ends.
There are 4 independent parts, one for each index of `cx`. The reference program is written for one: setup_inputs(seed, part) draws one part's arguments, and reference() takes and returns one part's arrays. A program takes and returns all parts, laid end to end along the dimension named above; an argument that names none is the same for every part. Nothing has to cross between parts.
All inputs are finite; a program needn't handle non-finite values.
Results may differ from the reference program's by a relative error of at most 0.013.
Values may be sent and summed in bfloat16 or wider, within the bound.
A program may use at most 64 MiB of HBM per device.

```python
import math
import jax
import jax.numpy as jnp
from jax import lax

HOMOLOG_DEPTH = 256
FACTOR_BREADTH = 32
PAIR_WIDTH = 128
HIDDEN_WIDTH = 512
HOMOLOG_TALLY = 32
RESIDUE_SPAN = 256


def level_of(stream_key, extent, shards, smallest, high):
    def one(position, blocks):
        heights = jax.random.uniform(jax.random.fold_in(jax.random.fold_in(stream_key, 6), position), (blocks,), jnp.float32, smallest / len(shards), high / len(shards))
        return jnp.repeat(jnp.exp(heights), extent[position] // blocks).reshape((-1,) + (1,) * (len(extent) - position - 1))

    gain = one(*shards[0])
    for cut in shards[1:]:
        gain = gain * one(*cut)
    return gain


def scatter_about(key, dims, width, bound, split=(), kind=jnp.bfloat16):
    gain = level_of(key, dims, split, -0.22, 0.18) if split else 1.0
    array = jax.random.normal(key, dims, jnp.float32) * width * gain
    return jnp.minimum(jnp.maximum(array, -bound), bound).astype(kind)


def setup_inputs(seed: int = 0, part: int = 0) -> dict:
    splits = jax.random.split(jax.random.key(seed), 10)
    part_splits = jax.random.split(jax.random.fold_in(splits[9], part), 10)
    return {
        "homolog_representation": scatter_about(part_splits[0], (HOMOLOG_TALLY, RESIDUE_SPAN, HOMOLOG_DEPTH), 1.0, 6.0, ((1, 128),)),
        "pairwise_representation": scatter_about(part_splits[1], (RESIDUE_SPAN, RESIDUE_SPAN, PAIR_WIDTH), 1.0, 6.0, ((0, 128),)),
        "pairwise_refreshed_adjoint": scatter_about(part_splits[2], (RESIDUE_SPAN, RESIDUE_SPAN, PAIR_WIDTH), 1.0, 6.0, ((0, 128),)),
        "homolog_standard_multiplier": jnp.clip(jnp.exp(jax.random.uniform(splits[3], (HOMOLOG_DEPTH,), jnp.float32, math.log(0.5), math.log(2.0))), 0.5, 2.0),
        "pairwise_standard_multiplier": jnp.clip(jnp.exp(jax.random.uniform(splits[4], (PAIR_WIDTH,), jnp.float32, math.log(0.5), math.log(2.0))), 0.5, 2.0),
        "paired_linear_operators": scatter_about(splits[5], (HOMOLOG_DEPTH, 2 * FACTOR_BREADTH), HOMOLOG_DEPTH ** -0.5, 0.375),
        "closing_linear_operator": scatter_about(splits[6], (FACTOR_BREADTH * FACTOR_BREADTH, PAIR_WIDTH), (FACTOR_BREADTH * FACTOR_BREADTH // 16) ** -0.5, 0.75),
        "widening_transition_weights": scatter_about(splits[7], (PAIR_WIDTH, HIDDEN_WIDTH), PAIR_WIDTH ** -0.5, 0.5),
        "narrowing_transition_weights": scatter_about(splits[8], (HIDDEN_WIDTH, PAIR_WIDTH), HIDDEN_WIDTH ** -0.5, 0.25),
    }


EPSILON = 1e-05

def centered_homolog_entries(values, norm_gain):
    center = values - lax.optimization_barrier(jnp.mean(values, axis=-1, keepdims=True))
    spread_recip_factor = lax.rsqrt(lax.optimization_barrier(jnp.mean(center * center, axis=-1, keepdims=True)) + EPSILON)
    rescaled_homolog_entries = center * spread_recip_factor
    return (rescaled_homolog_entries * norm_gain, rescaled_homolog_entries, spread_recip_factor)

def standardize_adjoint_pass(d_normed, norm_gain, rescaled_homolog_entries, spread_recip_factor):
    d_unit = d_normed * norm_gain
    return spread_recip_factor * (d_unit - lax.optimization_barrier(jnp.mean(d_unit, axis=-1, keepdims=True)) - rescaled_homolog_entries * lax.optimization_barrier(jnp.mean(d_unit * rescaled_homolog_entries, axis=-1, keepdims=True)))

def lead_dot(left_mat, right_mat):
    return lax.dot_general(left_mat, right_mat, (((0,), (0,)), ((), ())), preferred_element_type=jnp.float32)

def backward_product(values, weight):
    return lax.dot_general(values, weight, (((values.ndim - 1,), (1,)), ((), ())), preferred_element_type=jnp.float32)

def pair_row(left_single_row, right_gathered, pair_in, cot_row, pairwise_standard_multiplier, closing_linear_operator, widening_transition_weights, narrowing_transition_weights):
    sequence_slice = left_single_row.shape[0]
    amino_index = right_gathered.shape[1]
    projected_channels = left_single_row.shape[1]
    right_single32 = right_gathered.astype(jnp.float32)
    outer_tensor = jnp.einsum('nr,nxg->xrg', left_single_row.astype(jnp.float32), right_single32) / sequence_slice
    outer_tensor = outer_tensor.reshape(amino_index, projected_channels * projected_channels).astype(jnp.bfloat16)
    update = jnp.dot(outer_tensor, closing_linear_operator, preferred_element_type=jnp.float32)
    middle = pair_in.astype(jnp.float32) + update
    centered_operand, rescaled_homolog_entries, spread_recip_factor = centered_homolog_entries(middle, pairwise_standard_multiplier)
    centered_operand = centered_operand.astype(jnp.bfloat16)
    pre_act = jnp.dot(centered_operand, widening_transition_weights, preferred_element_type=jnp.float32)
    sigmoid_gate = jax.nn.sigmoid(pre_act)
    active = (pre_act * sigmoid_gate).astype(jnp.bfloat16)
    result = (middle + jnp.dot(active, narrowing_transition_weights, preferred_element_type=jnp.float32)).astype(jnp.bfloat16)
    d_active = backward_product(cot_row, narrowing_transition_weights)
    d_pre = (d_active * sigmoid_gate * (1.0 + pre_act * (1.0 - sigmoid_gate))).astype(jnp.bfloat16)
    d_normed = backward_product(d_pre, widening_transition_weights)
    d_middle = (cot_row.astype(jnp.float32) + standardize_adjoint_pass(d_normed, pairwise_standard_multiplier, rescaled_homolog_entries, spread_recip_factor)).astype(jnp.bfloat16)
    outer_gradient = backward_product(d_middle, closing_linear_operator).astype(jnp.bfloat16)
    outer_gradient3 = outer_gradient.reshape(amino_index, projected_channels, projected_channels).astype(jnp.float32)
    left_gradient = (jnp.einsum('xua,dxa->du', outer_gradient3, right_single32) / sequence_slice).astype(jnp.bfloat16)
    col_part = jnp.einsum('sc,jce->sje', left_single_row.astype(jnp.float32), outer_gradient3)
    row_grads = (lead_dot(outer_tensor, d_middle), lead_dot(centered_operand, d_pre), lead_dot(active, cot_row))
    return (result, d_middle, left_gradient, col_part, row_grads)

def reference(homolog_representation, pairwise_representation, pairwise_refreshed_adjoint, homolog_standard_multiplier, pairwise_standard_multiplier, paired_linear_operators, closing_linear_operator, widening_transition_weights, narrowing_transition_weights):
    sequence_slice = homolog_representation.shape[0]
    amino_index = homolog_representation.shape[1]
    projected_channels = paired_linear_operators.shape[1] // 2
    centered_operand, rescaled_homolog_entries, spread_recip_factor = centered_homolog_entries(homolog_representation.astype(jnp.float32), homolog_standard_multiplier)
    centered_operand = centered_operand.astype(jnp.bfloat16)
    flat_rows = centered_operand.reshape(-1, centered_operand.shape[-1])
    projected_rows = jnp.dot(flat_rows, paired_linear_operators, preferred_element_type=jnp.float32).astype(jnp.bfloat16)
    projected_rows = projected_rows.reshape(sequence_slice, amino_index, 2 * projected_channels)
    left_proj = projected_rows[..., :projected_channels]
    right_gathered = projected_rows[..., projected_channels:]

    def row_step(accumulated_sums, inputs):
        left_single_row, pair_in, cot_row = inputs
        result, d_middle, left_gradient, col_part, row_grads = pair_row(left_single_row, right_gathered, pair_in, cot_row, pairwise_standard_multiplier, closing_linear_operator, widening_transition_weights, narrowing_transition_weights)
        accumulated_sums = (accumulated_sums[0] + row_grads[0], accumulated_sums[1] + row_grads[1], accumulated_sums[2] + row_grads[2], accumulated_sums[3] + col_part)
        return (accumulated_sums, (result, d_middle, left_gradient))
    initial_sums = (jnp.zeros(closing_linear_operator.shape, jnp.float32), jnp.zeros(widening_transition_weights.shape, jnp.float32), jnp.zeros(narrowing_transition_weights.shape, jnp.float32), jnp.zeros((sequence_slice, amino_index, projected_channels), jnp.float32))
    accumulated_sums, (pair_output, pair_gradient, d_lefts) = lax.scan(row_step, initial_sums, (jnp.swapaxes(left_proj, 0, 1), pairwise_representation, pairwise_refreshed_adjoint))
    right_gradient = (accumulated_sums[3] / sequence_slice).astype(jnp.bfloat16)
    left_gradient = jnp.swapaxes(d_lefts, 0, 1)
    projection_gradient = jnp.concatenate([left_gradient, right_gradient], axis=-1)
    projection_weight_gradient = lead_dot(flat_rows, projection_gradient.reshape(-1, 2 * projected_channels))
    homolog_standard_slope = backward_product(projection_gradient, paired_linear_operators)
    homolog_array_slope = standardize_adjoint_pass(homolog_standard_slope, homolog_standard_multiplier, rescaled_homolog_entries, spread_recip_factor).astype(jnp.bfloat16)
    return (pair_output, pair_gradient, homolog_array_slope, accumulated_sums[0] / amino_index, projection_weight_gradient / amino_index, accumulated_sums[1] / amino_index, accumulated_sums[2] / amino_index)
```

```python
import functools

import jax
import jax.numpy as jnp
from jax import lax
from jax.experimental import pallas as pl
from jax.experimental.pallas import tpu as pltpu
from jax.sharding import PartitionSpec as P

EPSILON = 1e-05
F32 = jnp.float32
BF16 = jnp.bfloat16
MESH = pl.DeviceIdType.MESH


def dot(a, b, ca=1, cb=0):
    return lax.dot_general(a, b, (((ca,), (cb,)), ((), ())), preferred_element_type=F32)


def layer_norm_parts(values):
    center = values - jnp.mean(values, axis=-1, keepdims=True)
    scale = lax.rsqrt(jnp.mean(center * center, axis=-1, keepdims=True) + EPSILON)
    return center * scale, scale


def layer_norm_adjoint(d_normed, gain, unit, scale):
    e = d_normed * gain
    return scale * (
        e
        - jnp.mean(e, axis=-1, keepdims=True)
        - unit * jnp.mean(e * unit, axis=-1, keepdims=True)
    )


def factor_index(block):
    return (block % 4) * 8 + block // 4


def main_kernel(
    dims,
    msa_hbm, pair_hbm, cot_hbm, gm_ref, gp_ref, wp_ref, wc_hbm, ww_hbm, wn_hbm,
    pair_out_hbm, pair_grad_hbm, msa_grad_ref, weights_ref, proj_ref,
    msa, pair, cot, wc, ww, wn,
    wcf, wide, m_mat, d_act, xn, unit_m, scale_m, left, left_t,
    own, gathered, gathered_f, r_mat,
    pn, active, d_pre, g_mat, res_out, grad_out_rows, dm_wide,
    d_part, d_recv, d_mid, d_recv2,
    w_part, w_recv, w_mid, w_recv2, w_own, w_all,
    p_part, p_recv, p_mid, p_recv2, p_own, p_all,
    load_sem, store_sem, z_send, z_recv, xy_send, xy_recv,
):
    ny, nz, nx = dims
    np_ = ny * nx
    n = np_ * nz
    me = lax.axis_index("res")
    x = lax.rem(me, nx)
    z = lax.rem(me // nx, nz)
    y = me // (nx * nz)
    p = y * nx + x

    def z_device(zz):
        return {"res": (y * nz + zz) * nx + x}

    def xy_device(pp):
        return {"res": ((pp // nx) * nz + z) * nx + lax.rem(pp, nx)}

    barrier = pltpu.get_barrier_semaphore()

    @pl.loop(1, nz)
    def _(k):
        pl.semaphore_signal(barrier, inc=1, device_id=z_device(lax.rem(z + k, nz)), device_id_type=MESH)

    @pl.loop(1, np_)
    def _(k):
        pl.semaphore_signal(barrier, inc=1, device_id=xy_device(lax.rem(p + k, np_)), device_id_type=MESH)

    loads = [
        pltpu.make_async_copy(src, dst, load_sem.at[i])
        for i, (src, dst) in enumerate(
            [(msa_hbm, msa), (wc_hbm, wc), (cot_hbm, cot), (wn_hbm, wn), (ww_hbm, ww), (pair_hbm, pair)]
        )
    ]
    for load in loads:
        load.start()

    def z_copy(stage, src, dst, zz, slot):
        return pltpu.make_async_remote_copy(
            src_ref=src, dst_ref=dst, send_sem=z_send.at[stage, zz], recv_sem=z_recv.at[stage, slot],
            device_id=z_device(zz), device_id_type=MESH)

    def xy_copy(stage, src, dst, pp, slot):
        return pltpu.make_async_remote_copy(
            src_ref=src, dst_ref=dst, send_sem=xy_send.at[stage, pp], recv_sem=xy_recv.at[stage, slot],
            device_id=xy_device(pp), device_id_type=MESH)

    def z_start(stage, src, dst):
        @pl.loop(1, nz)
        def _(k):
            zz = lax.rem(z + k, nz)
            z_copy(stage, src(zz), dst(z), zz, z).start()

    def z_wait(stage, src, dst):
        @pl.loop(1, nz)
        def _(k):
            zz = lax.rem(z + k, nz)
            z_copy(stage, src(zz), dst(zz), zz, zz).wait_recv()

    def z_done(stage, src, dst):
        @pl.loop(1, nz)
        def _(k):
            zz = lax.rem(z + k, nz)
            z_copy(stage, src(zz), dst(zz), zz, zz).wait_send()

    def xy_start(stage, src, dst):
        @pl.loop(1, np_)
        def _(k):
            pp = lax.rem(p + k, np_)
            xy_copy(stage, src(pp), dst(p), pp, p).start()

    def xy_wait(stage, src, dst):
        @pl.loop(1, np_)
        def _(k):
            pp = lax.rem(p + k, np_)
            xy_copy(stage, src(pp), dst(pp), pp, pp).wait_recv()

    def xy_done(stage, src, dst):
        @pl.loop(1, np_)
        def _(k):
            pp = lax.rem(p + k, np_)
            xy_copy(stage, src(pp), dst(pp), pp, pp).wait_send()

    def slab(ref, pp):
        return ref.at[pp // nx, :, lax.rem(pp, nx)]

    zs = {
        "gather": (0, lambda zz: own, lambda s: gathered.at[y, s, x]),
        "d": (1, lambda zz: d_mid.at[zz], lambda s: d_recv2.at[s]),
        "w": (2, lambda zz: w_mid.at[zz], lambda s: w_recv2.at[s]),
        "w_all": (3, lambda zz: w_own, lambda s: w_all.at[p, s]),
        "p": (4, lambda zz: p_mid, lambda s: p_recv2.at[s]),
    }
    xys = {
        "gather": (0, lambda pp: slab(gathered, p), lambda s: slab(gathered, s)),
        "d": (1, lambda pp: slab(d_part, pp), lambda s: d_recv.at[s]),
        "w": (2, lambda pp: w_part.at[pp], lambda s: w_recv.at[s]),
        "w_all": (3, lambda pp: w_all.at[p], lambda s: w_all.at[s]),
        "p": (4, lambda pp: p_part.at[pp], lambda s: p_recv.at[s]),
        "p_all": (5, lambda pp: p_own, lambda s: p_all.at[s]),
    }

    loads[0].wait()
    rows = jnp.concatenate([msa[:, 0, :].astype(F32), msa[:, 1, :].astype(F32)], axis=0)
    unit, scale = layer_norm_parts(rows)
    unit_m[...] = unit
    scale_m[...] = jnp.broadcast_to(scale, scale_m.shape)
    normed = (unit * gm_ref[...]).astype(BF16)
    xn[...] = normed
    proj_t = dot(wp_ref[...], normed, 1, 1)
    right_t = proj_t[32:64]
    own_f = jnp.concatenate(
        [
            jnp.concatenate([right_t[t * 8 : (t + 1) * 8, b * 32 : (b + 1) * 32] for t in range(4)], axis=1)
            for b in range(2)
        ],
        axis=0,
    )
    own[...] = own_f.astype(BF16)
    gathered[y, z, x] = own_f.astype(BF16)
    pl.semaphore_wait(barrier, nz - 1 + np_ - 1)
    z_start(*zs["gather"])

    left_t[...] = proj_t[0:32].astype(BF16)
    left[...] = dot(normed, wp_ref[0:32, :], 1, 1).astype(BF16)

    z_wait(*zs["gather"])
    xy_start(*xys["gather"])

    loads[1].wait()
    wcf[...] = wc[...].astype(F32)
    for block in range(32):
        wide[:, block * 128 : (block + 1) * 128] = wcf[pl.ds(factor_index(block), 32, stride=32), :].astype(BF16)
    for block in range(32):
        part = dot(left[...], wide[:, block * 128 : (block + 1) * 128]) * (1.0 / 32.0)
        for b in range(2):
            m_mat[block * 32 : (block + 1) * 32, b * 128 : (b + 1) * 128] = part[b * 32 : (b + 1) * 32].astype(BF16)
    loads[2].wait()
    loads[3].wait()
    for b in range(2):
        d_act[b] = dot(cot[b], wn[...], 1, 1)
    loads[4].wait()
    loads[5].wait()

    xy_wait(*xys["gather"])
    gathered_f[...] = gathered[...].reshape(n * 16, 128).astype(F32)
    for q in range(8):
        r_mat[:, q * 128 : (q + 1) * 128] = gathered_f[pl.ds(q, 2 * n, stride=8), :].astype(BF16)

    update = dot(r_mat[...], m_mat[...])
    gain_p = gp_ref[...]
    for b in range(2):
        middle = pair[b].astype(F32) + update[:, b * 128 : (b + 1) * 128]
        unit, scale = layer_norm_parts(middle)
        normed = (unit * gain_p).astype(BF16)
        pn[b] = normed
        pre = dot(normed, ww[...])
        gate = jax.nn.sigmoid(pre)
        act_f = pre * gate
        act = act_f.astype(BF16)
        active[b] = act
        res_out[b] = (middle + dot(act, wn[...])).astype(BF16)
        dp = (d_act[b] * (gate + act_f * (1.0 - gate))).astype(BF16)
        d_pre[b] = dp
        d_normed = dot(dp, ww[...], 1, 1)
        grad = (cot[b].astype(F32) + layer_norm_adjoint(d_normed, gain_p, unit, scale)).astype(BF16)
        grad_out_rows[b] = grad
        g_mat[:, b * 128 : (b + 1) * 128] = grad
    stores = [
        pltpu.make_async_copy(res_out, pair_out_hbm, store_sem.at[0]),
        pltpu.make_async_copy(grad_out_rows, pair_grad_hbm, store_sem.at[1]),
    ]
    for store in stores:
        store.start()

    for q in range(8):
        gathered_f[pl.ds(q, 2 * n, stride=8), :] = dot(g_mat[...], m_mat[q * 128 : (q + 1) * 128, :], 1, 1)
    d_part[...] = gathered_f[...].astype(BF16).reshape(d_part.shape)
    xy_start(*xys["d"])

    for block in range(8):
        dm = dot(r_mat[:, block * 128 : (block + 1) * 128], g_mat[...], 0, 0)
        for i in range(4):
            for b in range(2):
                dm_wide[b * 32 : (b + 1) * 32, (block * 4 + i) * 128 : (block * 4 + i + 1) * 128] = dm[
                    i * 32 : (i + 1) * 32, b * 128 : (b + 1) * 128
                ].astype(BF16)
    wrows = w_part.shape[1] * w_part.shape[2]

    def put(start, value):
        count = value.shape[0]
        height = w_part.shape[2]
        done = 0
        while done < count:
            first = start + done
            take = min(wrows - first % wrows, count - done)
            w_part[first // wrows, first % wrows // height : (first % wrows + take) // height] = (
                value[done : done + take].astype(BF16).reshape(take // height, height, 128)
            )
            done += take

    for block in range(32):
        if block % 8 == 0:
            go = dot(left_t[...], dm_wide[:, block * 128 : (block + 8) * 128]) * (1.0 / 32.0)
            go = jnp.concatenate([go[:, i * 128 : (i + 1) * 128] for i in range(8)], axis=0)
            put(block * 32, go)
    put(1024, dot(active[0], cot[0], 0, 0) + dot(active[1], cot[1], 0, 0))
    up = dot(pn[0], d_pre[0], 0, 0) + dot(pn[1], d_pre[1], 0, 0)
    put(1536, jnp.concatenate([up[:, i * 128 : (i + 1) * 128] for i in range(4)], axis=0))
    xy_start(*xys["w"])
    d_left_t = (dot(wide[...], dm_wide[...], 1, 1) * (1.0 / 32.0)).astype(BF16)

    d_recv[p] = d_part[y, :, x]
    xy_wait(*xys["d"])
    total = d_recv[0].astype(F32)
    for i in range(1, np_):
        total += d_recv[i].astype(F32)
    d_mid[...] = total.astype(BF16)
    z_start(*zs["d"])

    w_recv[p] = w_part[p]
    xy_wait(*xys["w"])
    total = w_recv[0].astype(F32)
    for i in range(1, np_):
        total += w_recv[i].astype(F32)
    w_mid[...] = total.astype(BF16)
    z_start(*zs["w"])

    d_recv2[z] = d_mid[z]
    z_wait(*zs["d"])
    total = d_recv2[0].astype(F32)
    for i in range(1, nz):
        total += d_recv2[i].astype(F32)
    d_right_t = jnp.concatenate(
        [
            jnp.concatenate([total[b * 8 : (b + 1) * 8, t * 32 : (t + 1) * 32] for t in range(4)], axis=0)
            for b in range(2)
        ],
        axis=1,
    ).astype(BF16)
    d_proj_t = jnp.concatenate([d_left_t, d_right_t], axis=0)
    pwg = dot(d_proj_t, xn[...])
    pwg = jnp.concatenate([pwg[:, 0:128], pwg[:, 128:256]], axis=0).astype(BF16)
    p_part[...] = pwg.reshape(p_part.shape)
    xy_start(*xys["p"])

    w_recv2[z] = w_mid[z]
    z_wait(*zs["w"])
    total = w_recv2[0].astype(F32)
    for i in range(1, nz):
        total += w_recv2[i].astype(F32)
    w_own[...] = total.astype(BF16)
    w_all[p, z] = total.astype(BF16)
    z_start(*zs["w_all"])

    p_recv[p] = p_part[p]
    xy_wait(*xys["p"])
    total = p_recv[0].astype(F32)
    for i in range(1, np_):
        total += p_recv[i].astype(F32)
    p_mid[...] = total.astype(BF16)
    p_recv2[z] = total.astype(BF16)
    z_start(*zs["p"])

    z_wait(*zs["w_all"])
    xy_start(*xys["w_all"])

    d_norm = dot(d_proj_t, wp_ref[...], 0, 0)
    slope = layer_norm_adjoint(d_norm, gm_ref[...], unit_m[...], scale_m[:, 0:1])
    msa_grad_ref[...] = slope.astype(BF16)

    z_wait(*zs["p"])
    total = p_recv2[0].astype(F32)
    for i in range(1, nz):
        total += p_recv2[i].astype(F32)
    p_own[...] = total.astype(BF16)
    p_all[p] = total.astype(BF16)
    xy_start(*xys["p_all"])
    xy_wait(*xys["w_all"])
    weights_ref[...] = w_all[...].reshape(weights_ref.shape)
    xy_wait(*xys["p_all"])
    proj_ref[...] = p_all[...].reshape(proj_ref.shape)

    for plan in zs.values():
        z_done(*plan)
    for plan in xys.values():
        xy_done(*plan)
    for store in stores:
        store.wait()


def final_kernel(
    pair_in, grad_in, msa_in, weights, proj,
    pair_out, grad_out_pair, msa_out, grad_out, proj_out, grad_up, grad_down,
    sem,
):
    copies = [
        pltpu.make_async_copy(pair_in, pair_out, sem.at[0]),
        pltpu.make_async_copy(grad_in, grad_out_pair, sem.at[1]),
    ]
    for copy in copies:
        copy.start()
    inv = 1.0 / 256.0
    for b in range(2):
        msa_out[:, b, :] = msa_in[b * 32 : (b + 1) * 32, :]
    for block in range(32):
        grad_out[pl.ds(factor_index(block), 32, stride=32), :] = (
            weights[block * 32 : (block + 1) * 32, :].astype(F32) * inv
        )
    grad_down[...] = weights[1024:1536, :].astype(F32) * inv
    for i in range(4):
        grad_up[:, i * 128 : (i + 1) * 128] = weights[1536 + i * 128 : 1536 + (i + 1) * 128, :].astype(F32) * inv
    for i in range(2):
        proj_out[:, i * 128 : (i + 1) * 128] = proj[i * 64 : (i + 1) * 64, :].astype(F32) * inv
    for copy in copies:
        copy.wait()


def local(dims, msa, pair, cot, gm, gp, wp, wc, ww, wn):
    ny, nz, nx = dims
    np_ = ny * nx
    n = np_ * nz
    wh = 2048 // n
    ph = 128 // np_
    hbm = pl.BlockSpec(memory_space=pl.ANY)
    vmem = pl.BlockSpec(memory_space=pltpu.VMEM)
    rows = pair.shape[1]

    def V(shape, dtype=BF16):
        return pltpu.VMEM(shape, dtype)

    scratch = [
        V((32, 2, 256)), V((2, rows, 128)), V((2, rows, 128)), V((1024, 128)), V((128, 512)), V((512, 128)),
        V((1024, 128), F32), V((32, 4096)), V((1024, 256)), V((2, rows, 512), F32), V((64, 256)),
        V((64, 256), F32), V((64, 128), F32), V((64, 32)), V((32, 64)),
        V((16, 128)), V((ny, nz, nx, 16, 128)), V((n * 16, 128), F32), V((rows, 1024)),
        V((2, rows, 128)), V((2, rows, 512)), V((2, rows, 512)), V((rows, 256)), V((2, rows, 128)),
        V((2, rows, 128)), V((64, 4096)),
        V((ny, nz, nx, 16, 128)), V((np_, nz, 16, 128)), V((nz, 16, 128)), V((nz, 16, 128)),
        V((np_, nz, wh, 128)), V((np_, nz, wh, 128)), V((nz, wh, 128)), V((nz, wh, 128)), V((wh, 128)),
        V((np_, nz, wh, 128)),
        V((np_, ph, 128)), V((np_, ph, 128)), V((ph, 128)), V((nz, ph, 128)), V((ph, 128)), V((np_, ph, 128)),
        pltpu.SemaphoreType.DMA((6,)),
        pltpu.SemaphoreType.DMA((2,)),
        pltpu.SemaphoreType.DMA((5, nz)),
        pltpu.SemaphoreType.DMA((5, nz)),
        pltpu.SemaphoreType.DMA((6, np_)),
        pltpu.SemaphoreType.DMA((6, np_)),
    ]
    outs = pl.pallas_call(
        functools.partial(main_kernel, dims),
        out_shape=[
            jax.ShapeDtypeStruct(pair.shape, BF16),
            jax.ShapeDtypeStruct(pair.shape, BF16),
            jax.ShapeDtypeStruct((64, 256), BF16),
            jax.ShapeDtypeStruct((2048, 128), BF16),
            jax.ShapeDtypeStruct((128, 128), BF16),
        ],
        in_specs=[hbm, hbm, hbm, vmem, vmem, vmem, hbm, hbm, hbm],
        out_specs=[hbm, hbm, vmem, vmem, vmem],
        scratch_shapes=scratch,
        compiler_params=pltpu.CompilerParams(
            collective_id=0, has_side_effects=True, vmem_limit_bytes=40 * 2**20
        ),
    )(msa, pair, cot, gm.reshape(1, -1), gp.reshape(1, -1), wp.T, wc, ww, wn)
    results = pl.pallas_call(
        final_kernel,
        out_shape=[
            jax.ShapeDtypeStruct(pair.shape, BF16),
            jax.ShapeDtypeStruct(pair.shape, BF16),
            jax.ShapeDtypeStruct(msa.shape, BF16),
            jax.ShapeDtypeStruct((1024, 128), F32),
            jax.ShapeDtypeStruct((64, 256), F32),
            jax.ShapeDtypeStruct((128, 512), F32),
            jax.ShapeDtypeStruct((512, 128), F32),
        ],
        in_specs=[hbm, hbm, vmem, vmem, vmem],
        out_specs=[hbm, hbm, vmem, vmem, vmem, vmem, vmem],
        scratch_shapes=[pltpu.SemaphoreType.DMA((2,))],
        compiler_params=pltpu.CompilerParams(vmem_limit_bytes=16 * 2**20),
    )(*outs)
    return tuple(r.T if i == 4 else r for i, r in enumerate(results))


DIMS = (2, 16, 4)


def solution(mesh, dims=DIMS):
    pairs = P(("cx", "res"), None, None)
    return jax.shard_map(
        functools.partial(local, dims),
        mesh=mesh,
        in_specs=(P("cx", "res", None), pairs, pairs, P(), P(), P(), P(), P(), P()),
        out_specs=(pairs, pairs, P("cx", "res", None), P("cx", None), P("cx", None), P("cx", None), P("cx", None)),
        check_vma=False,
    )
```

```python
import functools

import jax
import jax.numpy as jnp
from jax import lax
from jax.experimental import pallas as pl
from jax.experimental.pallas import tpu as pltpu
from jax.sharding import PartitionSpec as P

EPSILON = 1e-05
F32 = jnp.float32
BF16 = jnp.bfloat16
MESH = pl.DeviceIdType.MESH


def dot(a, b, ca=1, cb=0):
    return lax.dot_general(a, b, (((ca,), (cb,)), ((), ())), preferred_element_type=F32)


def layer_norm_parts(values):
    center = values - jnp.mean(values, axis=-1, keepdims=True)
    scale = lax.rsqrt(jnp.mean(center * center, axis=-1, keepdims=True) + EPSILON)
    return center * scale, scale


def layer_norm_adjoint(d_normed, gain, unit, scale):
    e = d_normed * gain
    return scale * (
        e
        - jnp.mean(e, axis=-1, keepdims=True)
        - unit * jnp.mean(e * unit, axis=-1, keepdims=True)
    )


def factor_index(block):
    return (block % 4) * 8 + block // 4


def main_kernel(
    dims,
    msa_hbm, pair_hbm, cot_hbm, gm_hbm, gp_hbm, wp_hbm, wc_hbm, ww_hbm, wn_hbm,
    res_out, grad_rows, msa_grad_ref, weights_ref, proj_ref,
    msa, gm_ref, gp_ref, wp_ref, pair, cot, wc, ww, wn,
    wcf, wide, m_mat, d_act, xn_col, unit_m, scale_m, left, left_t,
    own, gathered, flat, r_mat,
    pn, active, d_pre, g_mat, dm_wide,
    d_part, d_recv, d_mid, d_recv2,
    w_part, w_recv, w_mid, w_recv2, w_own, w_all,
    p_part, p_recv, p_mid, p_recv2, p_own, p_all,
    load_sem, z_send, z_recv, q_send, q_recv, xy_send, xy_recv, a_send, a_recv,
):
    ny, nq, nb, nx = dims
    nz = nq * nb
    np_ = ny * nx
    na = np_ * nb
    n = np_ * nz
    half = nz // 4
    me = lax.axis_index("res")
    x = lax.rem(me, nx)
    z = lax.rem(me // nx, nz)
    y = me // (nx * nz)
    q = z // nb
    b_ = lax.rem(z, nb)
    p = y * nx + x
    a = (y * nb + b_) * nx + x

    def at(yy, zz, xx):
        return {"res": (yy * nz + zz) * nx + xx}

    def z_device(zz):
        return at(y, zz, x)

    def q_device(qq):
        return at(y, qq * nb + b_, x)

    def xy_device(pp):
        return at(pp // nx, z, lax.rem(pp, nx))

    def a_device(aa):
        return at(aa // (nb * nx), q * nb + lax.rem(aa // nx, nb), lax.rem(aa, nx))

    loads = [
        pltpu.make_async_copy(src, dst, load_sem.at[i])
        for i, (src, dst) in enumerate(
            [
                (msa_hbm, msa), (gm_hbm, gm_ref), (wp_hbm, wp_ref), (wc_hbm, wc), (cot_hbm, cot),
                (wn_hbm, wn), (ww_hbm, ww), (pair_hbm, pair), (gp_hbm, gp_ref),
            ]
        )
    ]
    for load in loads[0:3]:
        load.start()

    def far_first(i):
        return lax.rem(z + nz // 2 + (1 - 2 * lax.rem(i, 2)) * ((i + 1) // 2), nz)

    barrier = pltpu.get_barrier_semaphore()

    @pl.loop(0, nz - 1)
    def _(i):
        pl.semaphore_signal(barrier, inc=1, device_id=z_device(far_first(i)), device_id_type=MESH)

    @pl.loop(1, np_)
    def _(k):
        pl.semaphore_signal(barrier, inc=1, device_id=xy_device(lax.rem(p + k, np_)), device_id_type=MESH)

    for load in loads[3:]:
        load.start()

    class Exchange:
        def __init__(self, axis, stage, src, dst):
            self.stage, self.src, self.dst = stage, src, dst
            self.device, self.count, self.mine, self.send, self.recv, self.peer = {
                "z": (z_device, nz, z, z_send, z_recv, lambda i: far_first(i - 1)),
                "q": (q_device, nq, q, q_send, q_recv, lambda i: lax.rem(q + i, nq)),
                "xy": (xy_device, np_, p, xy_send, xy_recv, lambda i: lax.rem(p + i, np_)),
                "a": (a_device, na, a, a_send, a_recv, lambda i: lax.rem(a + i, na)),
            }[axis]
            plans.append(self)

        def copy(self, to, slot, dst):
            return pltpu.make_async_remote_copy(
                src_ref=self.src(to), dst_ref=dst,
                send_sem=self.send.at[self.stage, to], recv_sem=self.recv.at[self.stage, slot],
                device_id=self.device(to), device_id_type=MESH)

        def start(self):
            @pl.loop(1, self.count)
            def _(i):
                to = self.peer(i)
                self.copy(to, self.mine, self.dst(to, self.mine)).start()

        def wait(self, first=1, last=None):
            @pl.loop(first, self.count if last is None else last)
            def _(i):
                slot = self.peer(i)
                self.copy(slot, slot, self.dst(self.mine, slot)).wait_recv()

        def done(self):
            @pl.loop(1, self.count)
            def _(i):
                to = self.peer(i)
                self.copy(to, to, self.dst(self.mine, to)).wait_send()

    plans = []

    def slot_of(at_z, from_z):
        return lax.rem(from_z - at_z + half + nz, nz)

    near = 2 * half + 1
    x_z = Exchange("z", 0, lambda to: own, lambda at_z, s: gathered.at[y, slot_of(at_z, s), x])
    x_near = Exchange(
        "xy", 0, lambda to: gathered.at[y, 0:near, x],
        lambda _, s: gathered.at[s // nx, 0:near, lax.rem(s, nx)])
    x_far = Exchange(
        "xy", 1, lambda to: gathered.at[y, near:nz, x],
        lambda _, s: gathered.at[s // nx, near:nz, lax.rem(s, nx)])
    x_norm = Exchange("q", 0, lambda to: xn_col.at[q], lambda _, s: xn_col.at[s])
    x_d = Exchange(
        "a", 0, lambda to: d_part.at[to // (nb * nx), :, lax.rem(to // nx, nb), lax.rem(to, nx)],
        lambda _, s: d_recv.at[s])
    x_d2 = Exchange("q", 1, lambda to: d_mid.at[to], lambda _, s: d_recv2.at[s])
    x_w = Exchange("a", 1, lambda to: w_part.at[to], lambda _, s: w_recv.at[s])
    x_w2 = Exchange("q", 2, lambda to: w_mid, lambda _, s: w_recv2.at[s])
    x_w3 = Exchange("a", 2, lambda to: w_own, lambda _, s: w_all.at[s])
    x_p = Exchange("xy", 2, lambda to: p_part.at[to], lambda _, s: p_recv.at[s])
    x_p2 = Exchange("z", 1, lambda to: p_mid, lambda _, s: p_recv2.at[s])
    x_p3 = Exchange("xy", 3, lambda to: p_own, lambda _, s: p_all.at[s])

    def summed(ref, count):
        total = ref[0].astype(F32)
        for i in range(1, count):
            total += ref[i].astype(F32)
        return total

    for load in loads[0:3]:
        load.wait()
    rows = jnp.concatenate([msa[:, 0, :].astype(F32), msa[:, 1, :].astype(F32)], axis=0)
    unit, scale = layer_norm_parts(rows)
    unit_m[...] = unit
    scale_m[...] = jnp.broadcast_to(scale, scale_m.shape)
    normed = (unit * gm_ref[...]).astype(BF16)
    proj_t = dot(wp_ref[...], normed, 1, 1)
    right_t = proj_t[32:64]
    own_f = jnp.concatenate(
        [
            jnp.concatenate([right_t[t * 8 : (t + 1) * 8, b * 32 : (b + 1) * 32] for t in range(4)], axis=1)
            for b in range(2)
        ],
        axis=0,
    )
    own[...] = own_f.astype(BF16)
    xn_col[q] = normed
    pl.semaphore_wait(barrier, nz - 1 + np_ - 1)
    x_z.start()
    x_norm.start()

    gathered[y, half, x] = own_f.astype(BF16)
    left_t[...] = proj_t[0:32].astype(BF16)
    left[...] = dot(normed, wp_ref[0:32, :], 1, 1).astype(BF16)
    loads[3].wait()
    wcf[...] = wc[...].astype(F32)
    for block in range(32):
        wide[:, block * 128 : (block + 1) * 128] = wcf[pl.ds(factor_index(block), 32, stride=32), :].astype(BF16)
    for block in range(32):
        part = dot(left[...], wide[:, block * 128 : (block + 1) * 128]) * (1.0 / 32.0)
        for b in range(2):
            m_mat[block * 32 : (block + 1) * 32, b * 128 : (b + 1) * 128] = part[b * 32 : (b + 1) * 32].astype(BF16)

    x_z.wait(nz - 2 * half)
    x_near.start()
    loads[4].wait()
    loads[5].wait()
    for b in range(2):
        d_act[b] = dot(cot[b], wn[...], 1, 1)
    for load in loads[6:9]:
        load.wait()
    x_z.wait(1, nz - 2 * half)
    x_far.start()

    x_near.wait()
    x_far.wait()
    for zz in range(nz):
        block = gathered[:, pl.ds(slot_of(z, zz), 1)]
        for yy in range(ny):
            flat[pl.ds((yy * nz + zz) * nx * 16, nx * 16), :] = block[yy].reshape(nx * 16, 128).astype(F32)
    for g in range(8):
        r_mat[:, g * 128 : (g + 1) * 128] = flat[pl.ds(g, 2 * n, stride=8), :].astype(BF16)

    update = dot(r_mat[...], m_mat[...])
    gain_p = gp_ref[...]
    for b in range(2):
        middle = pair[b].astype(F32) + update[:, b * 128 : (b + 1) * 128]
        unit, scale = layer_norm_parts(middle)
        normed = (unit * gain_p).astype(BF16)
        pn[b] = normed
        pre = dot(normed, ww[...])
        gate = jax.nn.sigmoid(pre)
        act_f = pre * gate
        act = act_f.astype(BF16)
        active[b] = act
        res_out[b] = (middle + dot(act, wn[...])).astype(BF16)
        dp = (d_act[b] * (gate + act_f * (1.0 - gate))).astype(BF16)
        d_pre[b] = dp
        d_normed = dot(dp, ww[...], 1, 1)
        grad = (cot[b].astype(F32) + layer_norm_adjoint(d_normed, gain_p, unit, scale)).astype(BF16)
        grad_rows[b] = grad
        g_mat[:, b * 128 : (b + 1) * 128] = grad

    for g in range(8):
        flat[pl.ds(g, 2 * n, stride=8), :] = dot(g_mat[...], m_mat[g * 128 : (g + 1) * 128, :], 1, 1)
    d_part[...] = flat[...].astype(BF16).reshape(d_part.shape)
    x_d.start()

    for block in range(8):
        dm = dot(r_mat[:, block * 128 : (block + 1) * 128], g_mat[...], 0, 0)
        for i in range(4):
            for b in range(2):
                dm_wide[b * 32 : (b + 1) * 32, (block * 4 + i) * 128 : (block * 4 + i + 1) * 128] = dm[
                    i * 32 : (i + 1) * 32, b * 128 : (b + 1) * 128
                ].astype(BF16)
    height = w_part.shape[1]

    def put(first, value):
        for i in range(0, value.shape[0], 32):
            piece, row = divmod(first + i, height)
            w_part[piece, row : row + 32] = value[i : i + 32].astype(BF16)

    for block in range(4):
        go = dot(left_t[...], dm_wide[:, block * 1024 : (block + 1) * 1024]) * (1.0 / 32.0)
        for i in range(8):
            put((block * 8 + i) * 32, go[:, i * 128 : (i + 1) * 128])
    put(1024, dot(active[0], cot[0], 0, 0) + dot(active[1], cot[1], 0, 0))
    up = dot(pn[0], d_pre[0], 0, 0) + dot(pn[1], d_pre[1], 0, 0)
    for i in range(4):
        put(1536 + i * 128, up[:, i * 128 : (i + 1) * 128])
    x_w.start()
    d_left_t = (dot(wide[...], dm_wide[...], 1, 1) * (1.0 / 32.0)).astype(BF16)
    p_left = dot(d_left_t, xn_col[q])

    def transposed(block):
        return jnp.concatenate(
            [
                jnp.concatenate([block[b * 8 : (b + 1) * 8, t * 32 : (t + 1) * 32] for t in range(4)], axis=0)
                for b in range(2)
            ],
            axis=1,
        ).astype(BF16)

    x_norm.wait()
    d_recv[a] = d_part[y, :, b_, x]
    x_d.wait()
    total = summed(d_recv, na)
    d_mid[...] = total.astype(BF16)
    x_d2.start()
    p_right = dot(transposed(total[0]), xn_col[0])
    for i in range(1, nq):
        p_right += dot(transposed(total[i]), xn_col[i])
    pwg = jnp.concatenate([p_left, p_right], axis=0)
    pwg = jnp.concatenate([pwg[:, 0:128], pwg[:, 128:256]], axis=0).astype(BF16)
    p_part[...] = pwg.reshape(p_part.shape)
    x_p.start()

    w_recv[a] = w_part[a]
    x_w.wait()
    total = summed(w_recv, na).astype(BF16)
    w_mid[...] = total
    x_w2.start()
    w_recv2[q] = total

    p_recv[p] = p_part[p]
    x_p.wait()
    total = summed(p_recv, np_).astype(BF16)
    p_mid[...] = total
    x_p2.start()
    p_recv2[z] = total

    x_w2.wait()
    total = summed(w_recv2, nq).astype(BF16)
    w_own[...] = total
    x_w3.start()
    w_all[a] = total

    d_recv2[q] = d_mid[q]
    x_d2.wait()
    d_proj_t = jnp.concatenate([d_left_t, transposed(summed(d_recv2, nq))], axis=0)
    d_norm = dot(d_proj_t, wp_ref[...], 0, 0)
    slope = layer_norm_adjoint(d_norm, gm_ref[...], unit_m[...], scale_m[:, 0:1])
    msa_grad_ref[...] = slope.astype(BF16)

    x_p2.wait()
    total = summed(p_recv2, nz).astype(BF16)
    p_own[...] = total
    x_p3.start()
    p_all[p] = total
    x_w3.wait()
    weights_ref[...] = w_all[...].reshape(weights_ref.shape)
    x_p3.wait()
    proj_ref[...] = p_all[...].reshape(proj_ref.shape)

    for plan in plans:
        plan.done()


def final_kernel(
    pair_in, grad_in, msa_in, weights, proj,
    pair_out, grad_out_pair, msa_out, grad_out, proj_out, grad_up, grad_down,
    sem,
):
    copies = [
        pltpu.make_async_copy(pair_in, pair_out, sem.at[0]),
        pltpu.make_async_copy(grad_in, grad_out_pair, sem.at[1]),
    ]
    for copy in copies:
        copy.start()
    inv = 1.0 / 256.0
    for b in range(2):
        msa_out[:, b, :] = msa_in[b * 32 : (b + 1) * 32, :]
    for block in range(32):
        grad_out[pl.ds(factor_index(block), 32, stride=32), :] = (
            weights[block * 32 : (block + 1) * 32, :].astype(F32) * inv
        )
    grad_down[...] = weights[1024:1536, :].astype(F32) * inv
    for i in range(4):
        grad_up[:, i * 128 : (i + 1) * 128] = weights[1536 + i * 128 : 1536 + (i + 1) * 128, :].astype(F32) * inv
    for i in range(2):
        proj_out[:, i * 128 : (i + 1) * 128] = proj[i * 64 : (i + 1) * 64, :].astype(F32) * inv
    for copy in copies:
        copy.wait()


def local(dims, msa, pair, cot, gm, gp, wp, wc, ww, wn):
    ny, nq, nb, nx = dims
    nz = nq * nb
    np_ = ny * nx
    na = np_ * nb
    n = np_ * nz
    wh = 2048 // na
    ph = 128 // np_
    hbm = pl.BlockSpec(memory_space=pltpu.HBM)
    vmem = pl.BlockSpec(memory_space=pltpu.VMEM)
    rows = pair.shape[1]

    def V(shape, dtype=BF16):
        return pltpu.VMEM(shape, dtype)

    D = pltpu.SemaphoreType.DMA
    scratch = [
        V((32, 2, 256)), V((1, 256), F32), V((1, 128), F32), V((64, 256)),
        V((2, rows, 128)), V((2, rows, 128)), V((1024, 128)), V((128, 512)), V((512, 128)),
        V((1024, 128), F32), V((32, 4096)), V((1024, 256)), V((2, rows, 512), F32), V((nq, 64, 256)),
        V((64, 256), F32), V((64, 128), F32), V((64, 32)), V((32, 64)),
        V((16, 128)), V((ny, nz, nx, 16, 128)), V((n * 16, 128), F32), V((rows, 1024)),
        V((2, rows, 128)), V((2, rows, 512)), V((2, rows, 512)), V((rows, 256)), V((64, 4096)),
        V((ny, nq, nb, nx, 16, 128)), V((na, nq, 16, 128)), V((nq, 16, 128)), V((nq, 16, 128)),
        V((na, wh, 128)), V((na, wh, 128)), V((wh, 128)), V((nq, wh, 128)), V((wh, 128)), V((na, wh, 128)),
        V((np_, ph, 128)), V((np_, ph, 128)), V((ph, 128)), V((nz, ph, 128)), V((ph, 128)), V((np_, ph, 128)),
        D((9,)), D((2, nz)), D((2, nz)), D((3, nq)), D((3, nq)), D((4, np_)), D((4, np_)), D((3, na)), D((3, na)),
    ]
    outs = pl.pallas_call(
        functools.partial(main_kernel, dims),
        out_shape=[
            jax.ShapeDtypeStruct(pair.shape, BF16),
            jax.ShapeDtypeStruct(pair.shape, BF16),
            jax.ShapeDtypeStruct((64, 256), BF16),
            jax.ShapeDtypeStruct((2048, 128), BF16),
            jax.ShapeDtypeStruct((128, 128), BF16),
        ],
        in_specs=[hbm] * 9,
        out_specs=[vmem] * 5,
        scratch_shapes=scratch,
        compiler_params=pltpu.CompilerParams(
            collective_id=0, has_side_effects=True, vmem_limit_bytes=40 * 2**20
        ),
    )(*[
        pltpu.with_memory_space_constraint(v, pltpu.HBM)
        for v in (msa, pair, cot, gm.reshape(1, -1), gp.reshape(1, -1), wp.T, wc, ww, wn)
    ])
    results = pl.pallas_call(
        final_kernel,
        out_shape=[
            jax.ShapeDtypeStruct(pair.shape, BF16),
            jax.ShapeDtypeStruct(pair.shape, BF16),
            jax.ShapeDtypeStruct(msa.shape, BF16),
            jax.ShapeDtypeStruct((1024, 128), F32),
            jax.ShapeDtypeStruct((64, 256), F32),
            jax.ShapeDtypeStruct((128, 512), F32),
            jax.ShapeDtypeStruct((512, 128), F32),
        ],
        in_specs=[vmem] * 5,
        out_specs=[pl.BlockSpec(memory_space=pltpu.HBM)] * 2 + [vmem] * 5,
        scratch_shapes=[pltpu.SemaphoreType.DMA((2,))],
        compiler_params=pltpu.CompilerParams(vmem_limit_bytes=16 * 2**20),
    )(*outs)
    return tuple(r.T if i == 4 else r for i, r in enumerate(results))


DIMS = (2, 4, 4, 4)


def solution(mesh, dims=DIMS):
    pairs = P(("cx", "res"), None, None)
    return jax.shard_map(
        functools.partial(local, dims),
        mesh=mesh,
        in_specs=(P("cx", "res", None), pairs, pairs, P(), P(), P(), P(), P(), P()),
        out_specs=(pairs, pairs, P("cx", "res", None), P("cx", None), P("cx", None), P("cx", None), P("cx", None)),
        check_vma=False,
    )
```

```python
import functools

import jax
import jax.numpy as jnp
from jax import lax
from jax.experimental import pallas as pl
from jax.experimental.pallas import tpu as pltpu
from jax.sharding import PartitionSpec as P

EPSILON = 1e-05
F32 = jnp.float32
BF16 = jnp.bfloat16
MESH = pl.DeviceIdType.MESH


def dot(a, b, ca=1, cb=0):
    return lax.dot_general(a, b, (((ca,), (cb,)), ((), ())), preferred_element_type=F32)


def layer_norm_parts(values):
    center = values - jnp.mean(values, axis=-1, keepdims=True)
    scale = lax.rsqrt(jnp.mean(center * center, axis=-1, keepdims=True) + EPSILON)
    return center * scale, scale


def layer_norm_adjoint(d_normed, gain, unit, scale):
    e = d_normed * gain
    return scale * (
        e
        - jnp.mean(e, axis=-1, keepdims=True)
        - unit * jnp.mean(e * unit, axis=-1, keepdims=True)
    )


def factor_index(block):
    return (block % 4) * 8 + block // 4


def main_kernel(
    dims,
    msa_hbm, pair_hbm, cot_hbm, gm_hbm, gp_hbm, wp_hbm, wc_hbm, ww_hbm, wn_hbm,
    res_out, grad_rows, msa_grad_ref, weights_ref, proj_ref,
    msa, gm_ref, gp_ref, wp_ref, pair, cot, wc, ww, wn,
    wcf, wide, m_mat, d_act, xn, unit_m, scale_m, left, left_t,
    own, gathered, flat, r_mat,
    pn, active, d_pre, g_mat, dm_wide,
    d_part, d_recv, d_mid, d_recv2,
    w_part, w_recv, w_mid, w_recv2, w_own, w_all,
    p_part, p_recv, p_mid, p_recv2, p_own, p_all,
    load_sem, z_send, z_recv, xy_send, xy_recv,
):
    ny, nz, nx = dims
    np_ = ny * nx
    n = np_ * nz
    half = nz // 4
    me = lax.axis_index("res")
    x = lax.rem(me, nx)
    z = lax.rem(me // nx, nz)
    y = me // (nx * nz)
    p = y * nx + x

    def at(yy, zz, xx):
        return {"res": (yy * nz + zz) * nx + xx}

    def z_device(zz):
        return at(y, zz, x)

    def xy_device(pp):
        return at(pp // nx, z, lax.rem(pp, nx))

    loads = [
        pltpu.make_async_copy(src, dst, load_sem.at[i])
        for i, (src, dst) in enumerate(
            [
                (msa_hbm, msa), (gm_hbm, gm_ref), (wp_hbm, wp_ref), (wc_hbm, wc), (cot_hbm, cot),
                (wn_hbm, wn), (ww_hbm, ww), (pair_hbm, pair), (gp_hbm, gp_ref),
            ]
        )
    ]
    for load in loads[0:3]:
        load.start()

    def far_first(i):
        return lax.rem(z + nz // 2 + (1 - 2 * lax.rem(i, 2)) * ((i + 1) // 2), nz)

    barrier = pltpu.get_barrier_semaphore()

    @pl.loop(0, nz - 1)
    def _(i):
        pl.semaphore_signal(barrier, inc=1, device_id=z_device(far_first(i)), device_id_type=MESH)

    @pl.loop(1, np_)
    def _(k):
        pl.semaphore_signal(barrier, inc=1, device_id=xy_device(lax.rem(p + k, np_)), device_id_type=MESH)

    for load in loads[3:]:
        load.start()

    class Exchange:
        def __init__(self, axis, stage, src, dst):
            self.stage, self.src, self.dst = stage, src, dst
            self.device, self.count, self.mine, self.send, self.recv, self.peer = {
                "z": (z_device, nz, z, z_send, z_recv, lambda i: far_first(i - 1)),
                "xy": (xy_device, np_, p, xy_send, xy_recv, lambda i: lax.rem(p + i, np_)),
            }[axis]

        def copy(self, to, slot, dst):
            return pltpu.make_async_remote_copy(
                src_ref=self.src(to), dst_ref=dst,
                send_sem=self.send.at[self.stage, to], recv_sem=self.recv.at[self.stage, slot],
                device_id=self.device(to), device_id_type=MESH)

        def start(self):
            @pl.loop(1, self.count)
            def _(i):
                to = self.peer(i)
                self.copy(to, self.mine, self.dst(to, self.mine)).start()

        def wait(self, first=1, last=None):
            @pl.loop(first, self.count if last is None else last)
            def _(i):
                slot = self.peer(i)
                self.copy(slot, slot, self.dst(self.mine, slot)).wait_recv()

        def done(self):
            @pl.loop(1, self.count)
            def _(i):
                to = self.peer(i)
                self.copy(to, to, self.dst(self.mine, to)).wait_send()

    def slot_of(at_z, from_z):
        return lax.rem(from_z - at_z + half + nz, nz)

    near = 2 * half + 1
    x_z = Exchange("z", 0, lambda to: own, lambda at_z, s: gathered.at[y, slot_of(at_z, s), x])
    x_near = Exchange(
        "xy", 0, lambda to: gathered.at[y, 0:near, x],
        lambda _, s: gathered.at[s // nx, 0:near, lax.rem(s, nx)])
    x_far = Exchange(
        "xy", 1, lambda to: gathered.at[y, near:nz, x],
        lambda _, s: gathered.at[s // nx, near:nz, lax.rem(s, nx)])
    x_d = Exchange("xy", 2, lambda to: d_part.at[to // nx, :, lax.rem(to, nx)], lambda _, s: d_recv.at[s])
    x_d2 = Exchange("z", 1, lambda to: d_mid.at[to], lambda _, s: d_recv2.at[s])
    x_w = Exchange("xy", 3, lambda to: w_part.at[to], lambda _, s: w_recv.at[s])
    x_w2 = Exchange("z", 2, lambda to: w_mid.at[to], lambda _, s: w_recv2.at[s])
    x_w3 = Exchange("z", 3, lambda to: w_own, lambda at_z, s: w_all.at[p, slot_of(at_z, s)])
    x_w_near = Exchange("xy", 4, lambda to: w_all.at[p, 0:near], lambda _, s: w_all.at[s, 0:near])
    x_w_far = Exchange("xy", 5, lambda to: w_all.at[p, near:nz], lambda _, s: w_all.at[s, near:nz])
    x_p = Exchange("xy", 6, lambda to: p_part.at[to], lambda _, s: p_recv.at[s])
    x_p2 = Exchange("z", 4, lambda to: p_mid, lambda _, s: p_recv2.at[s])
    x_p3 = Exchange("xy", 7, lambda to: p_own, lambda _, s: p_all.at[s])

    def summed(ref, count):
        total = ref[0].astype(F32)
        for i in range(1, count):
            total += ref[i].astype(F32)
        return total

    for load in loads[0:3]:
        load.wait()
    rows = jnp.concatenate([msa[:, 0, :].astype(F32), msa[:, 1, :].astype(F32)], axis=0)
    unit, scale = layer_norm_parts(rows)
    unit_m[...] = unit
    scale_m[...] = jnp.broadcast_to(scale, scale_m.shape)
    normed = (unit * gm_ref[...]).astype(BF16)
    proj_t = dot(wp_ref[...], normed, 1, 1)
    right_t = proj_t[32:64]
    own_f = jnp.concatenate(
        [
            jnp.concatenate([right_t[t * 8 : (t + 1) * 8, b * 32 : (b + 1) * 32] for t in range(4)], axis=1)
            for b in range(2)
        ],
        axis=0,
    )
    own[...] = own_f.astype(BF16)
    xn[...] = normed
    pl.semaphore_wait(barrier, nz - 1 + np_ - 1)
    x_z.start()

    gathered[y, half, x] = own_f.astype(BF16)
    left_t[...] = proj_t[0:32].astype(BF16)
    left[...] = dot(normed, wp_ref[0:32, :], 1, 1).astype(BF16)
    loads[3].wait()
    wcf[...] = wc[...].astype(F32)
    for block in range(32):
        wide[:, block * 128 : (block + 1) * 128] = wcf[pl.ds(factor_index(block), 32, stride=32), :].astype(BF16)
    for block in range(32):
        part = dot(left[...], wide[:, block * 128 : (block + 1) * 128]) * (1.0 / 32.0)
        for b in range(2):
            m_mat[block * 32 : (block + 1) * 32, b * 128 : (b + 1) * 128] = part[b * 32 : (b + 1) * 32].astype(BF16)

    x_z.wait(nz - 2 * half)
    x_near.start()
    loads[4].wait()
    loads[5].wait()
    for b in range(2):
        d_act[b] = dot(cot[b], wn[...], 1, 1)
    for load in loads[6:9]:
        load.wait()
    x_z.wait(1, nz - 2 * half)
    x_far.start()

    x_near.wait()
    x_far.wait()
    for zz in range(nz):
        block = gathered[:, pl.ds(slot_of(z, zz), 1)]
        for yy in range(ny):
            flat[pl.ds((yy * nz + zz) * nx * 16, nx * 16), :] = block[yy].reshape(nx * 16, 128).astype(F32)
    for g in range(8):
        r_mat[:, g * 128 : (g + 1) * 128] = flat[pl.ds(g, 2 * n, stride=8), :].astype(BF16)

    update = dot(r_mat[...], m_mat[...])
    gain_p = gp_ref[...]
    for b in range(2):
        middle = pair[b].astype(F32) + update[:, b * 128 : (b + 1) * 128]
        unit, scale = layer_norm_parts(middle)
        normed = (unit * gain_p).astype(BF16)
        pn[b] = normed
        pre = dot(normed, ww[...])
        gate = jax.nn.sigmoid(pre)
        act_f = pre * gate
        act = act_f.astype(BF16)
        active[b] = act
        res_out[b] = (middle + dot(act, wn[...])).astype(BF16)
        dp = (d_act[b] * (gate + act_f * (1.0 - gate))).astype(BF16)
        d_pre[b] = dp
        d_normed = dot(dp, ww[...], 1, 1)
        grad = (cot[b].astype(F32) + layer_norm_adjoint(d_normed, gain_p, unit, scale)).astype(BF16)
        grad_rows[b] = grad
        g_mat[:, b * 128 : (b + 1) * 128] = grad

    for g in range(8):
        flat[pl.ds(g, 2 * n, stride=8), :] = dot(g_mat[...], m_mat[g * 128 : (g + 1) * 128, :], 1, 1)
    d_part[...] = flat[...].astype(BF16).reshape(d_part.shape)
    x_d.start()

    for block in range(8):
        dm = dot(r_mat[:, block * 128 : (block + 1) * 128], g_mat[...], 0, 0)
        for i in range(4):
            for b in range(2):
                dm_wide[b * 32 : (b + 1) * 32, (block * 4 + i) * 128 : (block * 4 + i + 1) * 128] = dm[
                    i * 32 : (i + 1) * 32, b * 128 : (b + 1) * 128
                ].astype(BF16)
    slab, height = w_part.shape[1] * w_part.shape[2], w_part.shape[2]

    def put(first, value):
        for i in range(0, value.shape[0], 16):
            peer, row = divmod(first + i, slab)
            w_part[peer, row // height, row % height : row % height + 16] = value[i : i + 16].astype(BF16)

    for block in range(4):
        go = dot(left_t[...], dm_wide[:, block * 1024 : (block + 1) * 1024]) * (1.0 / 32.0)
        for i in range(8):
            put((block * 8 + i) * 32, go[:, i * 128 : (i + 1) * 128])
    put(1024, dot(active[0], cot[0], 0, 0) + dot(active[1], cot[1], 0, 0))
    up = dot(pn[0], d_pre[0], 0, 0) + dot(pn[1], d_pre[1], 0, 0)
    for i in range(4):
        put(1536 + i * 128, up[:, i * 128 : (i + 1) * 128])
    d_left_t = (dot(wide[...], dm_wide[...], 1, 1) * (1.0 / 32.0)).astype(BF16)

    def transposed(block):
        return jnp.concatenate(
            [
                jnp.concatenate([block[b * 8 : (b + 1) * 8, t * 32 : (t + 1) * 32] for t in range(4)], axis=0)
                for b in range(2)
            ],
            axis=1,
        ).astype(BF16)

    d_recv[p] = d_part[y, :, x]
    w_recv[p] = w_part[p]
    x_d.wait()
    total = summed(d_recv, np_).astype(BF16)
    d_mid[...] = total
    x_d2.start()
    x_w.start()
    d_recv2[z] = d_mid[z]

    x_w.wait()
    w_mid[...] = summed(w_recv, np_).astype(BF16)
    x_w2.start()
    w_recv2[z] = w_mid[z]

    x_d2.wait()
    d_proj_t = jnp.concatenate([d_left_t, transposed(summed(d_recv2, nz))], axis=0)
    pwg = dot(d_proj_t, xn[...])
    pwg = jnp.concatenate([pwg[:, 0:128], pwg[:, 128:256]], axis=0).astype(BF16)
    p_part[...] = pwg.reshape(p_part.shape)
    x_p.start()
    p_recv[p] = p_part[p]
    d_norm = dot(d_proj_t, wp_ref[...], 0, 0)
    slope = layer_norm_adjoint(d_norm, gm_ref[...], unit_m[...], scale_m[:, 0:1])
    msa_grad_ref[...] = slope.astype(BF16)

    x_p.wait()
    total = summed(p_recv, np_).astype(BF16)
    p_mid[...] = total
    x_p2.start()
    p_recv2[z] = total

    for plan in (x_z, x_near, x_far, x_d, x_w):
        plan.done()

    x_w2.wait()
    total = summed(w_recv2, nz).astype(BF16)
    w_own[...] = total
    x_w3.start()
    w_all[p, half] = total

    x_w3.wait(nz - 2 * half)
    x_w_near.start()
    x_p2.wait()
    total = summed(p_recv2, nz).astype(BF16)
    p_own[...] = total
    x_p3.start()
    p_all[p] = total
    x_w3.wait(1, nz - 2 * half)
    x_w_far.start()
    for plan in (x_d2, x_p, x_w2, x_p2, x_w3):
        plan.done()
    x_p3.wait()
    proj_ref[...] = p_all[...].reshape(proj_ref.shape)
    x_w_near.wait()
    x_w_far.wait()
    for zz in range(nz):
        block = w_all[:, pl.ds(slot_of(z, zz), 1)]
        for pp in range(np_):
            weights_ref[pl.ds((pp * nz + zz) * height, height), :] = block[pp, 0]

    for plan in (x_p3, x_w_near, x_w_far):
        plan.done()


def final_kernel(
    pair_in, grad_in, msa_in, weights, proj,
    pair_out, grad_out_pair, msa_out, grad_out, proj_out, grad_up, grad_down,
    sem,
):
    copies = [
        pltpu.make_async_copy(pair_in, pair_out, sem.at[0]),
        pltpu.make_async_copy(grad_in, grad_out_pair, sem.at[1]),
    ]
    for copy in copies:
        copy.start()
    inv = 1.0 / 256.0
    for b in range(2):
        msa_out[:, b, :] = msa_in[b * 32 : (b + 1) * 32, :]
    for block in range(32):
        grad_out[pl.ds(factor_index(block), 32, stride=32), :] = (
            weights[block * 32 : (block + 1) * 32, :].astype(F32) * inv
        )
    grad_down[...] = weights[1024:1536, :].astype(F32) * inv
    for i in range(4):
        grad_up[:, i * 128 : (i + 1) * 128] = weights[1536 + i * 128 : 1536 + (i + 1) * 128, :].astype(F32) * inv
    for i in range(2):
        proj_out[:, i * 128 : (i + 1) * 128] = proj[i * 64 : (i + 1) * 64, :].astype(F32) * inv
    for copy in copies:
        copy.wait()


def local(dims, msa, pair, cot, gm, gp, wp, wc, ww, wn):
    ny, nz, nx = dims
    np_ = ny * nx
    n = np_ * nz
    wh = 2048 // n
    ph = 128 // np_
    hbm = pl.BlockSpec(memory_space=pltpu.HBM)
    vmem = pl.BlockSpec(memory_space=pltpu.VMEM)
    rows = pair.shape[1]

    def V(shape, dtype=BF16):
        return pltpu.VMEM(shape, dtype)

    D = pltpu.SemaphoreType.DMA
    scratch = [
        V((32, 2, 256)), V((1, 256), F32), V((1, 128), F32), V((64, 256)),
        V((2, rows, 128)), V((2, rows, 128)), V((1024, 128)), V((128, 512)), V((512, 128)),
        V((1024, 128), F32), V((32, 4096)), V((1024, 256)), V((2, rows, 512), F32), V((64, 256)),
        V((64, 256), F32), V((64, 128), F32), V((64, 32)), V((32, 64)),
        V((16, 128)), V((ny, nz, nx, 16, 128)), V((n * 16, 128), F32), V((rows, 1024)),
        V((2, rows, 128)), V((2, rows, 512)), V((2, rows, 512)), V((rows, 256)), V((64, 4096)),
        V((ny, nz, nx, 16, 128)), V((np_, nz, 16, 128)), V((nz, 16, 128)), V((nz, 16, 128)),
        V((np_, nz, wh, 128)), V((np_, nz, wh, 128)), V((nz, wh, 128)), V((nz, wh, 128)), V((wh, 128)),
        V((np_, nz, wh, 128)),
        V((np_, ph, 128)), V((np_, ph, 128)), V((ph, 128)), V((nz, ph, 128)), V((ph, 128)), V((np_, ph, 128)),
        D((9,)), D((5, nz)), D((5, nz)), D((8, np_)), D((8, np_)),
    ]
    outs = pl.pallas_call(
        functools.partial(main_kernel, dims),
        out_shape=[
            jax.ShapeDtypeStruct(pair.shape, BF16),
            jax.ShapeDtypeStruct(pair.shape, BF16),
            jax.ShapeDtypeStruct((64, 256), BF16),
            jax.ShapeDtypeStruct((2048, 128), BF16),
            jax.ShapeDtypeStruct((128, 128), BF16),
        ],
        in_specs=[hbm] * 9,
        out_specs=[vmem] * 5,
        scratch_shapes=scratch,
        compiler_params=pltpu.CompilerParams(
            collective_id=0, has_side_effects=True, vmem_limit_bytes=40 * 2**20
        ),
    )(*[
        pltpu.with_memory_space_constraint(v, pltpu.HBM)
        for v in (msa, pair, cot, gm.reshape(1, -1), gp.reshape(1, -1), wp.T, wc, ww, wn)
    ])
    results = pl.pallas_call(
        final_kernel,
        out_shape=[
            jax.ShapeDtypeStruct(pair.shape, BF16),
            jax.ShapeDtypeStruct(pair.shape, BF16),
            jax.ShapeDtypeStruct(msa.shape, BF16),
            jax.ShapeDtypeStruct((1024, 128), F32),
            jax.ShapeDtypeStruct((64, 256), F32),
            jax.ShapeDtypeStruct((128, 512), F32),
            jax.ShapeDtypeStruct((512, 128), F32),
        ],
        in_specs=[vmem] * 5,
        out_specs=[pl.BlockSpec(memory_space=pltpu.HBM)] * 2 + [vmem] * 5,
        scratch_shapes=[pltpu.SemaphoreType.DMA((2,))],
        compiler_params=pltpu.CompilerParams(vmem_limit_bytes=16 * 2**20),
    )(*outs)
    return tuple(r.T if i == 4 else r for i, r in enumerate(results))


DIMS = (2, 16, 4)


def solution(mesh, dims=DIMS):
    pairs = P(("cx", "res"), None, None)
    return jax.shard_map(
        functools.partial(local, dims),
        mesh=mesh,
        in_specs=(P("cx", "res", None), pairs, pairs, P(), P(), P(), P(), P(), P()),
        out_specs=(pairs, pairs, P("cx", "res", None), P("cx", None), P("cx", None), P("cx", None), P("cx", None)),
        check_vma=False,
    )
```

```python
import functools

import jax
import jax.numpy as jnp
from jax import lax
from jax.experimental import pallas as pl
from jax.experimental.pallas import tpu as pltpu
from jax.sharding import PartitionSpec as P

EPSILON = 1e-05
F32 = jnp.float32
BF16 = jnp.bfloat16
MESH = pl.DeviceIdType.MESH


def dot(a, b, ca=1, cb=0):
    return lax.dot_general(a, b, (((ca,), (cb,)), ((), ())), preferred_element_type=F32)


def layer_norm_parts(values):
    center = values - jnp.mean(values, axis=-1, keepdims=True)
    scale = lax.rsqrt(jnp.mean(center * center, axis=-1, keepdims=True) + EPSILON)
    return center * scale, scale


def layer_norm_adjoint(d_normed, gain, unit, scale):
    e = d_normed * gain
    return scale * (
        e
        - jnp.mean(e, axis=-1, keepdims=True)
        - unit * jnp.mean(e * unit, axis=-1, keepdims=True)
    )


def factor_index(block):
    return (block % 4) * 8 + block // 4


def main_kernel(
    dims,
    msa_hbm, pair_hbm, cot_hbm, gm_hbm, gp_hbm, wp_hbm, wc_hbm, ww_hbm, wn_hbm,
    res_out, grad_rows, msa_grad_ref, weights_ref, proj_ref,
    msa, gm_ref, gp_ref, wp_ref, pair, cot, wc, ww, wn,
    wcf, wide, m_mat, d_act, xn, unit_m, scale_m, left, left_t,
    own, gathered, flat, r_mat,
    pn, active, d_pre, g_mat, dm_wide,
    d_part, d_recv, d_mid, d_recv2,
    w_part, w_recv, w_mid, w_recv2, w_own, w_all,
    p_part, p_recv, p_mid, p_recv2, p_own, p_all,
    load_sem, z_send, z_recv, xy_send, xy_recv,
):
    ny, nz, nx = dims
    np_ = ny * nx
    n = np_ * nz
    half = nz // 4
    me = lax.axis_index("res")
    x = lax.rem(me, nx)
    z = lax.rem(me // nx, nz)
    y = me // (nx * nz)
    p = y * nx + x

    def at(yy, zz, xx):
        return {"res": (yy * nz + zz) * nx + xx}

    def z_device(zz):
        return at(y, zz, x)

    def xy_device(pp):
        return at(pp // nx, z, lax.rem(pp, nx))

    loads = [
        pltpu.make_async_copy(src, dst, load_sem.at[i])
        for i, (src, dst) in enumerate(
            [
                (msa_hbm, msa), (gm_hbm, gm_ref), (wp_hbm, wp_ref), (wc_hbm, wc), (cot_hbm, cot),
                (wn_hbm, wn), (ww_hbm, ww), (pair_hbm, pair), (gp_hbm, gp_ref),
            ]
        )
    ]
    def far_first(i):
        return lax.rem(z + nz // 2 + (1 - 2 * lax.rem(i, 2)) * ((i + 1) // 2), nz)

    barrier = pltpu.get_barrier_semaphore()

    @pl.loop(0, nz - 1)
    def _(i):
        pl.semaphore_signal(barrier, inc=1, device_id=z_device(far_first(i)), device_id_type=MESH)

    for load in loads[0:3]:
        load.start()

    @pl.loop(1, np_)
    def _(k):
        pl.semaphore_signal(barrier, inc=1, device_id=xy_device(lax.rem(p + k, np_)), device_id_type=MESH)

    for load in loads[3:]:
        load.start()

    class Exchange:
        def __init__(self, axis, stage, src, dst):
            self.stage, self.src, self.dst = stage, src, dst
            self.device, self.count, self.mine, self.send, self.recv, self.peer = {
                "z": (z_device, nz, z, z_send, z_recv, lambda i: far_first(i - 1)),
                "xy": (xy_device, np_, p, xy_send, xy_recv, lambda i: lax.rem(p + i, np_)),
            }[axis]

        def copy(self, to, slot, dst):
            return pltpu.make_async_remote_copy(
                src_ref=self.src(to), dst_ref=dst,
                send_sem=self.send.at[self.stage, to], recv_sem=self.recv.at[self.stage, slot],
                device_id=self.device(to), device_id_type=MESH)

        def start(self, first=1, last=None):
            @pl.loop(first, self.count if last is None else last)
            def _(i):
                to = self.peer(i)
                self.copy(to, self.mine, self.dst(to, self.mine)).start()

        def wait(self, first=1, last=None):
            @pl.loop(first, self.count if last is None else last)
            def _(i):
                slot = self.peer(i)
                self.copy(slot, slot, self.dst(self.mine, slot)).wait_recv()

        def done(self):
            @pl.loop(1, self.count)
            def _(i):
                to = self.peer(i)
                self.copy(to, to, self.dst(self.mine, to)).wait_send()

    def slot_of(at_z, from_z):
        return lax.rem(from_z - at_z + half + nz, nz)

    near = 2 * half + 1
    x_z = Exchange("z", 0, lambda to: own, lambda at_z, s: gathered.at[y, slot_of(at_z, s), x])
    x_near = Exchange(
        "xy", 0, lambda to: gathered.at[y, 0:near, x],
        lambda _, s: gathered.at[s // nx, 0:near, lax.rem(s, nx)])
    x_far = Exchange(
        "xy", 1, lambda to: gathered.at[y, near:nz, x],
        lambda _, s: gathered.at[s // nx, near:nz, lax.rem(s, nx)])
    x_d_far = Exchange(
        "xy", 2, lambda to: d_part.at[to // nx, near:nz, lax.rem(to, nx)], lambda _, s: d_recv.at[s, near:nz])
    x_d_near = Exchange(
        "xy", 8, lambda to: d_part.at[to // nx, 0:near, lax.rem(to, nx)], lambda _, s: d_recv.at[s, 0:near])
    x_d2 = Exchange("z", 1, lambda to: d_mid.at[slot_of(z, to)], lambda _, s: d_recv2.at[s])
    x_w1_far = Exchange("xy", 3, lambda to: w_part.at[to, near:nz], lambda _, s: w_recv.at[s, near:nz])
    x_w1_near = Exchange("xy", 9, lambda to: w_part.at[to, 0:near], lambda _, s: w_recv.at[s, 0:near])
    x_w2 = Exchange("z", 2, lambda to: w_mid.at[slot_of(z, to)], lambda _, s: w_recv2.at[s])
    x_w3 = Exchange("z", 3, lambda to: w_own, lambda at_z, s: w_all.at[p, slot_of(at_z, s)])
    x_w_near = Exchange("xy", 4, lambda to: w_all.at[p, 0:near], lambda _, s: w_all.at[s, 0:near])
    x_w_far = Exchange("xy", 5, lambda to: w_all.at[p, near:nz], lambda _, s: w_all.at[s, near:nz])
    x_p = Exchange("xy", 6, lambda to: p_part.at[to], lambda _, s: p_recv.at[s])
    x_p2 = Exchange("z", 4, lambda to: p_mid, lambda _, s: p_recv2.at[s])
    x_p3 = Exchange("xy", 7, lambda to: p_own, lambda _, s: p_all.at[s])

    def summed(ref, count, first=None, last=None):
        total = ref[0, first:last].astype(F32)
        for i in range(1, count):
            total += ref[i, first:last].astype(F32)
        return total

    for load in loads[0:3]:
        load.wait()
    rows = jnp.concatenate([msa[:, 0, :].astype(F32), msa[:, 1, :].astype(F32)], axis=0)
    unit, scale = layer_norm_parts(rows)
    unit_m[...] = unit
    scale_m[...] = jnp.broadcast_to(scale, scale_m.shape)
    normed = (unit * gm_ref[...]).astype(BF16)
    proj_t = dot(wp_ref[...], normed, 1, 1)
    right_t = proj_t[32:64]
    own_f = jnp.concatenate(
        [
            jnp.concatenate([right_t[t * 8 : (t + 1) * 8, b * 32 : (b + 1) * 32] for t in range(4)], axis=1)
            for b in range(2)
        ],
        axis=0,
    )
    own[...] = own_f.astype(BF16)
    xn[...] = normed
    pl.semaphore_wait(barrier, nz - 1 + np_ - 1)
    x_z.start()

    gathered[y, half, x] = own_f.astype(BF16)
    left_t[...] = proj_t[0:32].astype(BF16)
    left[...] = dot(normed, wp_ref[0:32, :], 1, 1).astype(BF16)
    loads[3].wait()
    wcf[...] = wc[...].astype(F32)
    for block in range(32):
        wide[:, block * 128 : (block + 1) * 128] = wcf[pl.ds(factor_index(block), 32, stride=32), :].astype(BF16)
    for block in range(32):
        part = dot(left[...], wide[:, block * 128 : (block + 1) * 128]) * (1.0 / 32.0)
        for b in range(2):
            m_mat[block * 32 : (block + 1) * 32, b * 128 : (b + 1) * 128] = part[b * 32 : (b + 1) * 32].astype(BF16)

    x_z.wait(nz - 2 * half)
    x_near.start()
    loads[4].wait()
    loads[5].wait()
    for b in range(2):
        d_act[b] = dot(cot[b], wn[...], 1, 1)
    for load in loads[6:9]:
        load.wait()
    x_z.wait(1, nz - 2 * half)
    x_far.start()

    x_near.wait()
    x_far.wait()
    for zz in range(nz):
        block = gathered[:, pl.ds(slot_of(z, zz), 1)]
        for yy in range(ny):
            flat[pl.ds((yy * nz + zz) * nx * 16, nx * 16), :] = block[yy].reshape(nx * 16, 128).astype(F32)
    for g in range(8):
        r_mat[:, g * 128 : (g + 1) * 128] = flat[pl.ds(g, 2 * n, stride=8), :].astype(BF16)

    update = dot(r_mat[...], m_mat[...])
    gain_p = gp_ref[...]
    for b in range(2):
        middle = pair[b].astype(F32) + update[:, b * 128 : (b + 1) * 128]
        unit, scale = layer_norm_parts(middle)
        normed = (unit * gain_p).astype(BF16)
        pn[b] = normed
        pre = dot(normed, ww[...])
        gate = jax.nn.sigmoid(pre)
        act_f = pre * gate
        act = act_f.astype(BF16)
        active[b] = act
        res_out[b] = (middle + dot(act, wn[...])).astype(BF16)
        dp = (d_act[b] * (gate + act_f * (1.0 - gate))).astype(BF16)
        d_pre[b] = dp
        d_normed = dot(dp, ww[...], 1, 1)
        grad = (cot[b].astype(F32) + layer_norm_adjoint(d_normed, gain_p, unit, scale)).astype(BF16)
        grad_rows[b] = grad
        g_mat[:, b * 128 : (b + 1) * 128] = grad

    for g in range(8):
        flat[pl.ds(g, 2 * n, stride=8), :] = dot(g_mat[...], m_mat[g * 128 : (g + 1) * 128, :], 1, 1)
    for zz in range(nz):
        for yy in range(ny):
            block = flat[(yy * nz + zz) * nx * 16 : (yy * nz + zz + 1) * nx * 16, :].astype(BF16)
            d_part[yy, slot_of(z, zz)] = block.reshape(nx, 16, 128)
    x_d_far.start()

    for block in range(8):
        dm = dot(r_mat[:, block * 128 : (block + 1) * 128], g_mat[...], 0, 0)
        for i in range(4):
            for b in range(2):
                dm_wide[b * 32 : (b + 1) * 32, (block * 4 + i) * 128 : (block * 4 + i + 1) * 128] = dm[
                    i * 32 : (i + 1) * 32, b * 128 : (b + 1) * 128
                ].astype(BF16)
    slab, height = w_part.shape[1] * w_part.shape[2], w_part.shape[2]

    def put(first, value):
        for i in range(0, value.shape[0], 16):
            peer, row = divmod(first + i, slab)
            w_part[peer, slot_of(z, row // height), row % height : row % height + 16] = value[i : i + 16].astype(BF16)

    for block in range(4):
        go = dot(left_t[...], dm_wide[:, block * 1024 : (block + 1) * 1024]) * (1.0 / 32.0)
        for i in range(8):
            put((block * 8 + i) * 32, go[:, i * 128 : (i + 1) * 128])
    put(1024, dot(active[0], cot[0], 0, 0) + dot(active[1], cot[1], 0, 0))
    up = dot(pn[0], d_pre[0], 0, 0) + dot(pn[1], d_pre[1], 0, 0)
    for i in range(4):
        put(1536 + i * 128, up[:, i * 128 : (i + 1) * 128])
    x_w1_far.start()
    d_left_t = (dot(wide[...], dm_wide[...], 1, 1) * (1.0 / 32.0)).astype(BF16)

    def transposed(block):
        return jnp.concatenate(
            [
                jnp.concatenate([block[b * 8 : (b + 1) * 8, t * 32 : (t + 1) * 32] for t in range(4)], axis=0)
                for b in range(2)
            ],
            axis=1,
        ).astype(BF16)

    d_recv[p] = d_part[y, :, x]
    w_recv[p] = w_part[p]
    far_end = nz - 2 * half
    x_d_far.wait()
    d_mid[near:nz] = summed(d_recv, np_, near, nz).astype(BF16)
    x_d2.start(1, far_end)
    x_d_near.start()
    x_w1_far.wait()
    w_mid[near:nz] = summed(w_recv, np_, near, nz).astype(BF16)
    x_w2.start(1, far_end)
    x_w1_near.start()
    x_d_near.wait()
    d_mid[0:near] = summed(d_recv, np_, 0, near).astype(BF16)
    x_d2.start(far_end)
    d_recv2[z] = d_mid[half]
    x_w1_near.wait()
    w_mid[0:near] = summed(w_recv, np_, 0, near).astype(BF16)
    x_w2.start(far_end)
    w_recv2[z] = w_mid[half]

    x_d2.wait()
    d_proj_t = jnp.concatenate([d_left_t, transposed(summed(d_recv2, nz))], axis=0)
    pwg = dot(d_proj_t, xn[...])
    pwg = jnp.concatenate([pwg[:, 0:128], pwg[:, 128:256]], axis=0).astype(BF16)
    p_part[...] = pwg.reshape(p_part.shape)
    x_p.start()
    p_recv[p] = p_part[p]
    d_norm = dot(d_proj_t, wp_ref[...], 0, 0)
    slope = layer_norm_adjoint(d_norm, gm_ref[...], unit_m[...], scale_m[:, 0:1])
    msa_grad_ref[...] = slope.astype(BF16)

    x_p.wait()
    total = summed(p_recv, np_).astype(BF16)
    p_mid[...] = total
    x_p2.start()
    p_recv2[z] = total

    for plan in (x_z, x_near, x_far, x_d_far, x_w1_far, x_d_near, x_w1_near):
        plan.done()

    x_w2.wait()
    total = summed(w_recv2, nz).astype(BF16)
    w_own[...] = total
    x_w3.start()
    w_all[p, half] = total

    x_w3.wait(nz - 2 * half)
    x_w_near.start()
    x_p2.wait()
    total = summed(p_recv2, nz).astype(BF16)
    p_own[...] = total
    x_p3.start()
    p_all[p] = total
    x_w3.wait(1, nz - 2 * half)
    x_w_far.start()
    for plan in (x_d2, x_p, x_w2, x_p2, x_w3):
        plan.done()
    x_p3.wait()
    proj_ref[...] = p_all[...].reshape(proj_ref.shape)
    x_w_near.wait()
    x_w_far.wait()
    for zz in range(nz):
        block = w_all[:, pl.ds(slot_of(z, zz), 1)]
        for pp in range(np_):
            weights_ref[pl.ds((pp * nz + zz) * height, height), :] = block[pp, 0]

    for plan in (x_p3, x_w_near, x_w_far):
        plan.done()


def final_kernel(
    pair_in, grad_in, msa_in, weights, proj,
    pair_out, grad_out_pair, msa_out, grad_out, proj_out, grad_up, grad_down,
    sem,
):
    copies = [
        pltpu.make_async_copy(pair_in, pair_out, sem.at[0]),
        pltpu.make_async_copy(grad_in, grad_out_pair, sem.at[1]),
    ]
    for copy in copies:
        copy.start()
    inv = 1.0 / 256.0
    for b in range(2):
        msa_out[:, b, :] = msa_in[b * 32 : (b + 1) * 32, :]
    for block in range(32):
        grad_out[pl.ds(factor_index(block), 32, stride=32), :] = (
            weights[block * 32 : (block + 1) * 32, :].astype(F32) * inv
        )
    grad_down[...] = weights[1024:1536, :].astype(F32) * inv
    for i in range(4):
        grad_up[:, i * 128 : (i + 1) * 128] = weights[1536 + i * 128 : 1536 + (i + 1) * 128, :].astype(F32) * inv
    for i in range(2):
        proj_out[:, i * 128 : (i + 1) * 128] = proj[i * 64 : (i + 1) * 64, :].astype(F32) * inv
    for copy in copies:
        copy.wait()


def local(dims, msa, pair, cot, gm, gp, wp, wc, ww, wn):
    ny, nz, nx = dims
    np_ = ny * nx
    n = np_ * nz
    wh = 2048 // n
    ph = 128 // np_
    hbm = pl.BlockSpec(memory_space=pltpu.HBM)
    vmem = pl.BlockSpec(memory_space=pltpu.VMEM)
    rows = pair.shape[1]

    def V(shape, dtype=BF16):
        return pltpu.VMEM(shape, dtype)

    D = pltpu.SemaphoreType.DMA
    scratch = [
        V((32, 2, 256)), V((1, 256), F32), V((1, 128), F32), V((64, 256)),
        V((2, rows, 128)), V((2, rows, 128)), V((1024, 128)), V((128, 512)), V((512, 128)),
        V((1024, 128), F32), V((32, 4096)), V((1024, 256)), V((2, rows, 512), F32), V((64, 256)),
        V((64, 256), F32), V((64, 128), F32), V((64, 32)), V((32, 64)),
        V((16, 128)), V((ny, nz, nx, 16, 128)), V((n * 16, 128), F32), V((rows, 1024)),
        V((2, rows, 128)), V((2, rows, 512)), V((2, rows, 512)), V((rows, 256)), V((64, 4096)),
        V((ny, nz, nx, 16, 128)), V((np_, nz, 16, 128)), V((nz, 16, 128)), V((nz, 16, 128)),
        V((np_, nz, wh, 128)), V((np_, nz, wh, 128)), V((nz, wh, 128)), V((nz, wh, 128)), V((wh, 128)),
        V((np_, nz, wh, 128)),
        V((np_, ph, 128)), V((np_, ph, 128)), V((ph, 128)), V((nz, ph, 128)), V((ph, 128)), V((np_, ph, 128)),
        D((9,)), D((5, nz)), D((5, nz)), D((10, np_)), D((10, np_)),
    ]
    outs = pl.pallas_call(
        functools.partial(main_kernel, dims),
        out_shape=[
            jax.ShapeDtypeStruct(pair.shape, BF16),
            jax.ShapeDtypeStruct(pair.shape, BF16),
            jax.ShapeDtypeStruct((64, 256), BF16),
            jax.ShapeDtypeStruct((2048, 128), BF16),
            jax.ShapeDtypeStruct((128, 128), BF16),
        ],
        in_specs=[hbm] * 9,
        out_specs=[vmem] * 5,
        scratch_shapes=scratch,
        compiler_params=pltpu.CompilerParams(
            collective_id=0, has_side_effects=True, vmem_limit_bytes=40 * 2**20
        ),
    )(*[
        pltpu.with_memory_space_constraint(v, pltpu.HBM)
        for v in (msa, pair, cot, gm.reshape(1, -1), gp.reshape(1, -1), wp.T, wc, ww, wn)
    ])
    results = pl.pallas_call(
        final_kernel,
        out_shape=[
            jax.ShapeDtypeStruct(pair.shape, BF16),
            jax.ShapeDtypeStruct(pair.shape, BF16),
            jax.ShapeDtypeStruct(msa.shape, BF16),
            jax.ShapeDtypeStruct((1024, 128), F32),
            jax.ShapeDtypeStruct((64, 256), F32),
            jax.ShapeDtypeStruct((128, 512), F32),
            jax.ShapeDtypeStruct((512, 128), F32),
        ],
        in_specs=[vmem] * 5,
        out_specs=[pl.BlockSpec(memory_space=pltpu.HBM)] * 2 + [vmem] * 5,
        scratch_shapes=[pltpu.SemaphoreType.DMA((2,))],
        compiler_params=pltpu.CompilerParams(vmem_limit_bytes=16 * 2**20),
    )(*outs)
    return tuple(r.T if i == 4 else r for i, r in enumerate(results))


DIMS = (2, 16, 4)


def solution(mesh, dims=DIMS):
    pairs = P(("cx", "res"), None, None)
    return jax.shard_map(
        functools.partial(local, dims),
        mesh=mesh,
        in_specs=(P("cx", "res", None), pairs, pairs, P(), P(), P(), P(), P(), P()),
        out_specs=(pairs, pairs, P("cx", "res", None), P("cx", None), P("cx", None), P("cx", None), P("cx", None)),
        check_vma=False,
    )
```

```python
import functools

import jax
import jax.numpy as jnp
from jax import lax
from jax.experimental import pallas as pl
from jax.experimental.pallas import tpu as pltpu
from jax.sharding import PartitionSpec as P

EPSILON = 1e-05
F32 = jnp.float32
BF16 = jnp.bfloat16
MESH = pl.DeviceIdType.MESH


def dot(a, b, ca=1, cb=0):
    return lax.dot_general(a, b, (((ca,), (cb,)), ((), ())), preferred_element_type=F32)


def layer_norm_parts(values):
    center = values - jnp.mean(values, axis=-1, keepdims=True)
    scale = lax.rsqrt(jnp.mean(center * center, axis=-1, keepdims=True) + EPSILON)
    return center * scale, scale


def layer_norm_adjoint(d_normed, gain, unit, scale):
    e = d_normed * gain
    return scale * (
        e
        - jnp.mean(e, axis=-1, keepdims=True)
        - unit * jnp.mean(e * unit, axis=-1, keepdims=True)
    )


def factor_index(block):
    return (block % 4) * 8 + block // 4


def main_kernel(
    dims,
    msa_hbm, pair_hbm, cot_hbm, gm_hbm, gp_hbm, wp_hbm, wc_hbm, ww_hbm, wn_hbm,
    res_out, grad_rows, msa_grad_ref, weights_ref, proj_ref,
    msa, gm_ref, gp_ref, wp_ref, pair, cot, wc, ww, wn,
    wcf, wide, m_mat, d_act, xn, unit_m, scale_m, left, left_t,
    own, gathered, flat, r_mat,
    pn, active, d_pre, g_mat, dm_wide,
    d_part, d_recv, d_mid, d_recv2,
    w_part, w_recv, w_mid, w_recv2, w_own, w_all,
    p_part, p_recv, p_mid, p_recv2, p_own, p_all,
    load_sem, z_send, z_recv, xy_send, xy_recv,
):
    ny, nz, nx = dims
    np_ = ny * nx
    n = np_ * nz
    half = nz // 4
    me = lax.axis_index("res")
    x = lax.rem(me, nx)
    z = lax.rem(me // nx, nz)
    y = me // (nx * nz)
    p = y * nx + x

    def at(yy, zz, xx):
        return {"res": (yy * nz + zz) * nx + xx}

    def z_device(zz):
        return at(y, zz, x)

    def xy_device(pp):
        return at(pp // nx, z, lax.rem(pp, nx))

    loads = [
        pltpu.make_async_copy(src, dst, load_sem.at[i])
        for i, (src, dst) in enumerate(
            [
                (msa_hbm, msa), (gm_hbm, gm_ref), (wp_hbm, wp_ref), (wc_hbm, wc), (cot_hbm, cot),
                (wn_hbm, wn), (ww_hbm, ww), (pair_hbm, pair), (gp_hbm, gp_ref),
            ]
        )
    ]
    def far_first(i):
        return lax.rem(z + nz // 2 + (1 - 2 * lax.rem(i, 2)) * ((i + 1) // 2), nz)

    barrier = pltpu.get_barrier_semaphore()

    @pl.loop(0, nz - 1)
    def _(i):
        pl.semaphore_signal(barrier, inc=1, device_id=z_device(far_first(i)), device_id_type=MESH)

    for load in loads[0:3]:
        load.start()

    @pl.loop(1, np_)
    def _(k):
        pl.semaphore_signal(barrier, inc=1, device_id=xy_device(lax.rem(p + k, np_)), device_id_type=MESH)

    for load in loads[3:]:
        load.start()

    class Exchange:
        def __init__(self, axis, stage, src, dst):
            self.stage, self.src, self.dst = stage, src, dst
            self.device, self.count, self.mine, self.send, self.recv, self.peer = {
                "z": (z_device, nz, z, z_send, z_recv, lambda i: far_first(i - 1)),
                "xy": (xy_device, np_, p, xy_send, xy_recv, lambda i: lax.rem(p + i, np_)),
            }[axis]

        def copy(self, to, slot, dst):
            return pltpu.make_async_remote_copy(
                src_ref=self.src(to), dst_ref=dst,
                send_sem=self.send.at[self.stage, to], recv_sem=self.recv.at[self.stage, slot],
                device_id=self.device(to), device_id_type=MESH)

        def start(self, first=1, last=None):
            @pl.loop(first, self.count if last is None else last)
            def _(i):
                to = self.peer(i)
                self.copy(to, self.mine, self.dst(to, self.mine)).start()

        def wait(self, first=1, last=None):
            @pl.loop(first, self.count if last is None else last)
            def _(i):
                slot = self.peer(i)
                self.copy(slot, slot, self.dst(self.mine, slot)).wait_recv()

        def done(self):
            @pl.loop(1, self.count)
            def _(i):
                to = self.peer(i)
                self.copy(to, to, self.dst(self.mine, to)).wait_send()

    def slot_of(at_z, from_z):
        return lax.rem(from_z - at_z + half + nz, nz)

    near = 2 * half + 1
    x_z = Exchange("z", 0, lambda to: own, lambda at_z, s: gathered.at[y, slot_of(at_z, s), x])
    x_near = Exchange(
        "xy", 0, lambda to: gathered.at[y, 0:near, x],
        lambda _, s: gathered.at[s // nx, 0:near, lax.rem(s, nx)])
    x_far = Exchange(
        "xy", 1, lambda to: gathered.at[y, near:nz, x],
        lambda _, s: gathered.at[s // nx, near:nz, lax.rem(s, nx)])
    x_d_far = Exchange(
        "xy", 2, lambda to: d_part.at[to // nx, near:nz, lax.rem(to, nx)], lambda _, s: d_recv.at[s, near:nz])
    x_d_near = Exchange(
        "xy", 8, lambda to: d_part.at[to // nx, 0:near, lax.rem(to, nx)], lambda _, s: d_recv.at[s, 0:near])
    x_d2 = Exchange("z", 1, lambda to: d_mid.at[slot_of(z, to)], lambda _, s: d_recv2.at[s])
    x_w1_far = Exchange("xy", 3, lambda to: w_part.at[to, near:nz], lambda _, s: w_recv.at[s, near:nz])
    x_w1_near = Exchange("xy", 9, lambda to: w_part.at[to, 0:near], lambda _, s: w_recv.at[s, 0:near])
    x_w2 = Exchange("z", 2, lambda to: w_mid.at[slot_of(z, to)], lambda _, s: w_recv2.at[s])
    x_w3 = Exchange("z", 3, lambda to: w_own, lambda at_z, s: w_all.at[p, slot_of(at_z, s)])
    x_w_near = Exchange("xy", 4, lambda to: w_all.at[p, 0:near], lambda _, s: w_all.at[s, 0:near])
    x_w_far = Exchange("xy", 5, lambda to: w_all.at[p, near:nz], lambda _, s: w_all.at[s, near:nz])
    x_p = Exchange("xy", 6, lambda to: p_part.at[to], lambda _, s: p_recv.at[s])
    x_p2 = Exchange("z", 4, lambda to: p_mid, lambda _, s: p_recv2.at[s])
    x_p3 = Exchange("xy", 7, lambda to: p_own, lambda _, s: p_all.at[s])

    def summed(ref, count, first=None, last=None):
        total = ref[0, first:last].astype(F32)
        for i in range(1, count):
            total += ref[i, first:last].astype(F32)
        return total

    for load in loads[0:3]:
        load.wait()
    rows = jnp.concatenate([msa[:, 0, :].astype(F32), msa[:, 1, :].astype(F32)], axis=0)
    unit, scale = layer_norm_parts(rows)
    unit_m[...] = unit
    scale_m[...] = jnp.broadcast_to(scale, scale_m.shape)
    normed = (unit * gm_ref[...]).astype(BF16)
    proj_t = dot(wp_ref[...], normed, 1, 1)
    right_t = proj_t[32:64]
    own_f = jnp.concatenate(
        [
            jnp.concatenate([right_t[t * 8 : (t + 1) * 8, b * 32 : (b + 1) * 32] for t in range(4)], axis=1)
            for b in range(2)
        ],
        axis=0,
    )
    own[...] = own_f.astype(BF16)
    xn[...] = normed
    pl.semaphore_wait(barrier, nz - 1 + np_ - 1)
    x_z.start()

    gathered[y, half, x] = own_f.astype(BF16)
    left_t[...] = proj_t[0:32].astype(BF16)
    left[...] = dot(normed, wp_ref[0:32, :], 1, 1).astype(BF16)
    loads[3].wait()
    wcf[...] = wc[...].astype(F32)
    for block in range(32):
        wide[:, block * 128 : (block + 1) * 128] = wcf[pl.ds(factor_index(block), 32, stride=32), :].astype(BF16)
    for block in range(32):
        part = dot(left[...], wide[:, block * 128 : (block + 1) * 128]) * (1.0 / 32.0)
        for b in range(2):
            m_mat[block * 32 : (block + 1) * 32, b * 128 : (b + 1) * 128] = part[b * 32 : (b + 1) * 32].astype(BF16)

    x_z.wait(nz - 2 * half)
    x_near.start()
    loads[4].wait()
    loads[5].wait()
    for b in range(2):
        d_act[b] = dot(cot[b], wn[...], 1, 1)
    for load in loads[6:9]:
        load.wait()
    x_z.wait(1, nz - 2 * half)
    x_far.start()

    x_near.wait()
    x_far.wait()
    for zz in range(nz):
        block = gathered[:, pl.ds(slot_of(z, zz), 1)]
        for yy in range(ny):
            flat[pl.ds((yy * nz + zz) * nx * 16, nx * 16), :] = block[yy].reshape(nx * 16, 128).astype(F32)
    for g in range(8):
        r_mat[:, g * 128 : (g + 1) * 128] = flat[pl.ds(g, 2 * n, stride=8), :].astype(BF16)

    update = dot(r_mat[...], m_mat[...])
    gain_p = gp_ref[...]
    for b in range(2):
        middle = pair[b].astype(F32) + update[:, b * 128 : (b + 1) * 128]
        unit, scale = layer_norm_parts(middle)
        normed = (unit * gain_p).astype(BF16)
        pn[b] = normed
        pre = dot(normed, ww[...])
        gate = jax.nn.sigmoid(pre)
        act_f = pre * gate
        act = act_f.astype(BF16)
        active[b] = act
        res_out[b] = (middle + dot(act, wn[...])).astype(BF16)
        dp = (d_act[b] * (gate + act_f * (1.0 - gate))).astype(BF16)
        d_pre[b] = dp
        d_normed = dot(dp, ww[...], 1, 1)
        grad = (cot[b].astype(F32) + layer_norm_adjoint(d_normed, gain_p, unit, scale)).astype(BF16)
        grad_rows[b] = grad
        g_mat[:, b * 128 : (b + 1) * 128] = grad

    for g in range(8):
        flat[pl.ds(g, 2 * n, stride=8), :] = dot(g_mat[...], m_mat[g * 128 : (g + 1) * 128, :], 1, 1)
    for zz in range(nz):
        for yy in range(ny):
            block = flat[(yy * nz + zz) * nx * 16 : (yy * nz + zz + 1) * nx * 16, :].astype(BF16)
            d_part[yy, slot_of(z, zz)] = block.reshape(nx, 16, 128)
    x_d_far.start()

    for block in range(8):
        dm = dot(r_mat[:, block * 128 : (block + 1) * 128], g_mat[...], 0, 0)
        for i in range(4):
            for b in range(2):
                dm_wide[b * 32 : (b + 1) * 32, (block * 4 + i) * 128 : (block * 4 + i + 1) * 128] = dm[
                    i * 32 : (i + 1) * 32, b * 128 : (b + 1) * 128
                ].astype(BF16)
    slab, height = w_part.shape[1] * w_part.shape[2], w_part.shape[2]

    def put(first, value):
        for i in range(0, value.shape[0], 16):
            peer, row = divmod(first + i, slab)
            w_part[peer, slot_of(z, row // height), row % height : row % height + 16] = value[i : i + 16].astype(BF16)

    for block in range(4):
        go = dot(left_t[...], dm_wide[:, block * 1024 : (block + 1) * 1024]) * (1.0 / 32.0)
        for i in range(8):
            put((block * 8 + i) * 32, go[:, i * 128 : (i + 1) * 128])
    put(1024, dot(active[0], cot[0], 0, 0) + dot(active[1], cot[1], 0, 0))
    up = dot(pn[0], d_pre[0], 0, 0) + dot(pn[1], d_pre[1], 0, 0)
    for i in range(4):
        put(1536 + i * 128, up[:, i * 128 : (i + 1) * 128])
    x_d_near.start()
    d_left_t = (dot(wide[...], dm_wide[...], 1, 1) * (1.0 / 32.0)).astype(BF16)

    def transposed(block):
        return jnp.concatenate(
            [
                jnp.concatenate([block[b * 8 : (b + 1) * 8, t * 32 : (t + 1) * 32] for t in range(4)], axis=0)
                for b in range(2)
            ],
            axis=1,
        ).astype(BF16)

    d_recv[p] = d_part[y, :, x]
    w_recv[p] = w_part[p]
    far_end = nz - 2 * half
    x_d_far.wait()
    d_mid[near:nz] = summed(d_recv, np_, near, nz).astype(BF16)
    x_d2.start(1, far_end)
    x_w1_far.start()
    x_d_near.wait()
    d_mid[0:near] = summed(d_recv, np_, 0, near).astype(BF16)
    x_d2.start(far_end)
    x_w1_near.start()
    d_recv2[z] = d_mid[half]
    x_w1_far.wait()
    w_mid[near:nz] = summed(w_recv, np_, near, nz).astype(BF16)
    x_w2.start(1, far_end)

    x_d2.wait()
    d_proj_t = jnp.concatenate([d_left_t, transposed(summed(d_recv2, nz))], axis=0)
    pwg = dot(d_proj_t, xn[...])
    pwg = jnp.concatenate([pwg[:, 0:128], pwg[:, 128:256]], axis=0).astype(BF16)
    p_part[...] = pwg.reshape(p_part.shape)
    x_p.start()

    x_w1_near.wait()
    w_mid[0:near] = summed(w_recv, np_, 0, near).astype(BF16)
    x_w2.start(far_end)
    w_recv2[z] = w_mid[half]

    p_recv[p] = p_part[p]
    d_norm = dot(d_proj_t, wp_ref[...], 0, 0)
    slope = layer_norm_adjoint(d_norm, gm_ref[...], unit_m[...], scale_m[:, 0:1])
    msa_grad_ref[...] = slope.astype(BF16)

    x_p.wait()
    total = summed(p_recv, np_).astype(BF16)
    p_mid[...] = total
    x_p2.start()
    p_recv2[z] = total

    for plan in (x_z, x_near, x_far, x_d_far, x_w1_far, x_d_near, x_w1_near):
        plan.done()

    x_w2.wait()
    total = summed(w_recv2, nz).astype(BF16)
    w_own[...] = total
    x_w3.start()
    w_all[p, half] = total

    x_w3.wait(nz - 2 * half)
    x_w_near.start()
    x_p2.wait()
    total = summed(p_recv2, nz).astype(BF16)
    p_own[...] = total
    x_p3.start()
    p_all[p] = total
    x_w3.wait(1, nz - 2 * half)
    x_w_far.start()
    for plan in (x_d2, x_p, x_w2, x_p2, x_w3):
        plan.done()
    x_p3.wait()
    proj_ref[...] = p_all[...].reshape(proj_ref.shape)
    x_w_near.wait()
    x_w_far.wait()
    for zz in range(nz):
        block = w_all[:, pl.ds(slot_of(z, zz), 1)]
        for pp in range(np_):
            weights_ref[pl.ds((pp * nz + zz) * height, height), :] = block[pp, 0]

    for plan in (x_p3, x_w_near, x_w_far):
        plan.done()


def final_kernel(
    pair_in, grad_in, msa_in, weights, proj,
    pair_out, grad_out_pair, msa_out, grad_out, proj_out, grad_up, grad_down,
    sem,
):
    copies = [
        pltpu.make_async_copy(pair_in, pair_out, sem.at[0]),
        pltpu.make_async_copy(grad_in, grad_out_pair, sem.at[1]),
    ]
    for copy in copies:
        copy.start()
    inv = 1.0 / 256.0
    for b in range(2):
        msa_out[:, b, :] = msa_in[b * 32 : (b + 1) * 32, :]
    for block in range(32):
        grad_out[pl.ds(factor_index(block), 32, stride=32), :] = (
            weights[block * 32 : (block + 1) * 32, :].astype(F32) * inv
        )
    grad_down[...] = weights[1024:1536, :].astype(F32) * inv
    for i in range(4):
        grad_up[:, i * 128 : (i + 1) * 128] = weights[1536 + i * 128 : 1536 + (i + 1) * 128, :].astype(F32) * inv
    for i in range(2):
        proj_out[:, i * 128 : (i + 1) * 128] = proj[i * 64 : (i + 1) * 64, :].astype(F32) * inv
    for copy in copies:
        copy.wait()


def local(dims, msa, pair, cot, gm, gp, wp, wc, ww, wn):
    ny, nz, nx = dims
    np_ = ny * nx
    n = np_ * nz
    wh = 2048 // n
    ph = 128 // np_
    hbm = pl.BlockSpec(memory_space=pltpu.HBM)
    vmem = pl.BlockSpec(memory_space=pltpu.VMEM)
    rows = pair.shape[1]

    def V(shape, dtype=BF16):
        return pltpu.VMEM(shape, dtype)

    D = pltpu.SemaphoreType.DMA
    scratch = [
        V((32, 2, 256)), V((1, 256), F32), V((1, 128), F32), V((64, 256)),
        V((2, rows, 128)), V((2, rows, 128)), V((1024, 128)), V((128, 512)), V((512, 128)),
        V((1024, 128), F32), V((32, 4096)), V((1024, 256)), V((2, rows, 512), F32), V((64, 256)),
        V((64, 256), F32), V((64, 128), F32), V((64, 32)), V((32, 64)),
        V((16, 128)), V((ny, nz, nx, 16, 128)), V((n * 16, 128), F32), V((rows, 1024)),
        V((2, rows, 128)), V((2, rows, 512)), V((2, rows, 512)), V((rows, 256)), V((64, 4096)),
        V((ny, nz, nx, 16, 128)), V((np_, nz, 16, 128)), V((nz, 16, 128)), V((nz, 16, 128)),
        V((np_, nz, wh, 128)), V((np_, nz, wh, 128)), V((nz, wh, 128)), V((nz, wh, 128)), V((wh, 128)),
        V((np_, nz, wh, 128)),
        V((np_, ph, 128)), V((np_, ph, 128)), V((ph, 128)), V((nz, ph, 128)), V((ph, 128)), V((np_, ph, 128)),
        D((9,)), D((5, nz)), D((5, nz)), D((10, np_)), D((10, np_)),
    ]
    outs = pl.pallas_call(
        functools.partial(main_kernel, dims),
        out_shape=[
            jax.ShapeDtypeStruct(pair.shape, BF16),
            jax.ShapeDtypeStruct(pair.shape, BF16),
            jax.ShapeDtypeStruct((64, 256), BF16),
            jax.ShapeDtypeStruct((2048, 128), BF16),
            jax.ShapeDtypeStruct((128, 128), BF16),
        ],
        in_specs=[hbm] * 9,
        out_specs=[vmem] * 5,
        scratch_shapes=scratch,
        compiler_params=pltpu.CompilerParams(
            collective_id=0, has_side_effects=True, vmem_limit_bytes=40 * 2**20
        ),
    )(*[
        pltpu.with_memory_space_constraint(v, pltpu.HBM)
        for v in (msa, pair, cot, gm.reshape(1, -1), gp.reshape(1, -1), wp.T, wc, ww, wn)
    ])
    results = pl.pallas_call(
        final_kernel,
        out_shape=[
            jax.ShapeDtypeStruct(pair.shape, BF16),
            jax.ShapeDtypeStruct(pair.shape, BF16),
            jax.ShapeDtypeStruct(msa.shape, BF16),
            jax.ShapeDtypeStruct((1024, 128), F32),
            jax.ShapeDtypeStruct((64, 256), F32),
            jax.ShapeDtypeStruct((128, 512), F32),
            jax.ShapeDtypeStruct((512, 128), F32),
        ],
        in_specs=[vmem] * 5,
        out_specs=[pl.BlockSpec(memory_space=pltpu.HBM)] * 2 + [vmem] * 5,
        scratch_shapes=[pltpu.SemaphoreType.DMA((2,))],
        compiler_params=pltpu.CompilerParams(vmem_limit_bytes=16 * 2**20),
    )(*outs)
    return tuple(r.T if i == 4 else r for i, r in enumerate(results))


DIMS = (2, 16, 4)


def solution(mesh, dims=DIMS):
    pairs = P(("cx", "res"), None, None)
    return jax.shard_map(
        functools.partial(local, dims),
        mesh=mesh,
        in_specs=(P("cx", "res", None), pairs, pairs, P(), P(), P(), P(), P(), P()),
        out_specs=(pairs, pairs, P("cx", "res", None), P("cx", None), P("cx", None), P("cx", None), P("cx", None)),
        check_vma=False,
    )
```

```python
import functools

import jax
import jax.numpy as jnp
from jax import lax
from jax.experimental import pallas as pl
from jax.experimental.pallas import tpu as pltpu
from jax.sharding import PartitionSpec as P

EPSILON = 1e-05
F32 = jnp.float32
BF16 = jnp.bfloat16
MESH = pl.DeviceIdType.MESH


def dot(a, b, ca=1, cb=0):
    return lax.dot_general(a, b, (((ca,), (cb,)), ((), ())), preferred_element_type=F32)


def layer_norm_parts(values):
    center = values - jnp.mean(values, axis=-1, keepdims=True)
    scale = lax.rsqrt(jnp.mean(center * center, axis=-1, keepdims=True) + EPSILON)
    return center * scale, scale


def layer_norm_adjoint(d_normed, gain, unit, scale):
    e = d_normed * gain
    return scale * (
        e
        - jnp.mean(e, axis=-1, keepdims=True)
        - unit * jnp.mean(e * unit, axis=-1, keepdims=True)
    )


def factor_index(block):
    return (block % 4) * 8 + block // 4


def main_kernel(
    dims,
    msa_hbm, pair_hbm, cot_hbm, gm_hbm, gp_hbm, wp_hbm, wc_hbm, ww_hbm, wn_hbm,
    res_out, grad_rows, msa_grad_ref, weights_ref, proj_ref,
    msa, gm_ref, gp_ref, wp_ref, pair, cot, wc, ww, wn,
    wcf, wide, m_mat, d_act, xn, unit_m, scale_m, left, left_t,
    own, gathered, flat, r_mat,
    pn, active, d_pre, g_mat, dm_wide,
    d_part, d_recv, d_mid, d_recv2,
    w_part, w_recv, w_mid, w_recv2, w_own, w_all,
    p_part, p_recv, p_mid, p_recv2, p_own, p_all,
    load_sem, z_send, z_recv, xy_send, xy_recv,
):
    ny, nz, nx = dims
    np_ = ny * nx
    n = np_ * nz
    half = nz // 4
    me = lax.axis_index("res")
    x = lax.rem(me, nx)
    z = lax.rem(me // nx, nz)
    y = me // (nx * nz)
    p = y * nx + x

    def at(yy, zz, xx):
        return {"res": (yy * nz + zz) * nx + xx}

    def z_device(zz):
        return at(y, zz, x)

    def xy_device(pp):
        return at(pp // nx, z, lax.rem(pp, nx))

    loads = [
        pltpu.make_async_copy(src, dst, load_sem.at[i])
        for i, (src, dst) in enumerate(
            [
                (msa_hbm, msa), (gm_hbm, gm_ref), (wp_hbm, wp_ref), (wc_hbm, wc), (cot_hbm, cot),
                (wn_hbm, wn), (ww_hbm, ww), (pair_hbm, pair), (gp_hbm, gp_ref),
            ]
        )
    ]
    def far_first(i):
        return lax.rem(z + nz // 2 + (1 - 2 * lax.rem(i, 2)) * ((i + 1) // 2), nz)

    barrier = pltpu.get_barrier_semaphore()

    @pl.loop(0, nz - 1, unroll=True)
    def _(i):
        pl.semaphore_signal(barrier, inc=1, device_id=z_device(far_first(i)), device_id_type=MESH)

    for load in loads[0:3]:
        load.start()

    @pl.loop(1, np_, unroll=True)
    def _(k):
        pl.semaphore_signal(barrier, inc=1, device_id=xy_device(lax.rem(p + k, np_)), device_id_type=MESH)

    for load in loads[3:]:
        load.start()

    class Exchange:
        def __init__(self, axis, stage, src, dst):
            self.stage, self.src, self.dst = stage, src, dst
            self.device, self.count, self.mine, self.send, self.recv, self.peer = {
                "z": (z_device, nz, z, z_send, z_recv, lambda i: far_first(i - 1)),
                "xy": (xy_device, np_, p, xy_send, xy_recv, lambda i: lax.rem(p + i, np_)),
            }[axis]

        def copy(self, to, slot, dst):
            return pltpu.make_async_remote_copy(
                src_ref=self.src(to), dst_ref=dst,
                send_sem=self.send.at[self.stage, to], recv_sem=self.recv.at[self.stage, slot],
                device_id=self.device(to), device_id_type=MESH)

        def start(self, first=1, last=None):
            @pl.loop(first, self.count if last is None else last, unroll=True)
            def _(i):
                to = self.peer(i)
                self.copy(to, self.mine, self.dst(to, self.mine)).start()

        def wait(self, first=1, last=None):
            @pl.loop(first, self.count if last is None else last, unroll=True)
            def _(i):
                slot = self.peer(i)
                self.copy(slot, slot, self.dst(self.mine, slot)).wait_recv()

        def done(self):
            @pl.loop(1, self.count, unroll=True)
            def _(i):
                to = self.peer(i)
                self.copy(to, to, self.dst(self.mine, to)).wait_send()

    def slot_of(at_z, from_z):
        return lax.rem(from_z - at_z + half + nz, nz)

    near = 2 * half + 1
    x_z = Exchange("z", 0, lambda to: own, lambda at_z, s: gathered.at[y, slot_of(at_z, s), x])
    x_near = Exchange(
        "xy", 0, lambda to: gathered.at[y, 0:near, x],
        lambda _, s: gathered.at[s // nx, 0:near, lax.rem(s, nx)])
    x_far = Exchange(
        "xy", 1, lambda to: gathered.at[y, near:nz, x],
        lambda _, s: gathered.at[s // nx, near:nz, lax.rem(s, nx)])
    x_d_far = Exchange(
        "xy", 2, lambda to: d_part.at[to // nx, near:nz, lax.rem(to, nx)], lambda _, s: d_recv.at[s, near:nz])
    x_d_near = Exchange(
        "xy", 8, lambda to: d_part.at[to // nx, 0:near, lax.rem(to, nx)], lambda _, s: d_recv.at[s, 0:near])
    x_d2 = Exchange("z", 1, lambda to: d_mid.at[slot_of(z, to)], lambda _, s: d_recv2.at[s])
    x_w1_far = Exchange("xy", 3, lambda to: w_part.at[to, near:nz], lambda _, s: w_recv.at[s, near:nz])
    x_w1_near = Exchange("xy", 9, lambda to: w_part.at[to, 0:near], lambda _, s: w_recv.at[s, 0:near])
    x_w2 = Exchange("z", 2, lambda to: w_mid.at[slot_of(z, to)], lambda _, s: w_recv2.at[s])
    x_w3 = Exchange("z", 3, lambda to: w_own, lambda at_z, s: w_all.at[p, slot_of(at_z, s)])
    x_w_near = Exchange("xy", 4, lambda to: w_all.at[p, 0:near], lambda _, s: w_all.at[s, 0:near])
    x_w_far = Exchange("xy", 5, lambda to: w_all.at[p, near:nz], lambda _, s: w_all.at[s, near:nz])
    x_p = Exchange("xy", 6, lambda to: p_part.at[to], lambda _, s: p_recv.at[s])
    x_p2 = Exchange("z", 4, lambda to: p_mid, lambda _, s: p_recv2.at[s])
    x_p3 = Exchange("xy", 7, lambda to: p_own, lambda _, s: p_all.at[s])

    def summed(ref, count, first=None, last=None):
        total = ref[0, first:last].astype(F32)
        for i in range(1, count):
            total += ref[i, first:last].astype(F32)
        return total

    for load in loads[0:3]:
        load.wait()
    rows = jnp.concatenate([msa[:, 0, :].astype(F32), msa[:, 1, :].astype(F32)], axis=0)
    unit, scale = layer_norm_parts(rows)
    unit_m[...] = unit
    scale_m[...] = jnp.broadcast_to(scale, scale_m.shape)
    normed = (unit * gm_ref[...]).astype(BF16)
    proj_t = dot(wp_ref[...], normed, 1, 1)
    right_t = proj_t[32:64]
    own_f = jnp.concatenate(
        [
            jnp.concatenate([right_t[t * 8 : (t + 1) * 8, b * 32 : (b + 1) * 32] for t in range(4)], axis=1)
            for b in range(2)
        ],
        axis=0,
    )
    own[...] = own_f.astype(BF16)
    xn[...] = normed
    pl.semaphore_wait(barrier, nz - 1 + np_ - 1)
    x_z.start()

    gathered[y, half, x] = own_f.astype(BF16)
    left_t[...] = proj_t[0:32].astype(BF16)
    left[...] = dot(normed, wp_ref[0:32, :], 1, 1).astype(BF16)
    loads[3].wait()
    wcf[...] = wc[...].astype(F32)
    for block in range(32):
        wide[:, block * 128 : (block + 1) * 128] = wcf[pl.ds(factor_index(block), 32, stride=32), :].astype(BF16)
    for block in range(32):
        part = dot(left[...], wide[:, block * 128 : (block + 1) * 128]) * (1.0 / 32.0)
        for b in range(2):
            m_mat[block * 32 : (block + 1) * 32, b * 128 : (b + 1) * 128] = part[b * 32 : (b + 1) * 32].astype(BF16)

    x_z.wait(nz - 2 * half)
    x_near.start()
    loads[4].wait()
    loads[5].wait()
    for b in range(2):
        d_act[b] = dot(cot[b], wn[...], 1, 1)
    for load in loads[6:9]:
        load.wait()
    x_z.wait(1, nz - 2 * half)
    x_far.start()

    x_near.wait()
    x_far.wait()
    for zz in range(nz):
        block = gathered[:, pl.ds(slot_of(z, zz), 1)]
        for yy in range(ny):
            flat[pl.ds((yy * nz + zz) * nx * 16, nx * 16), :] = block[yy].reshape(nx * 16, 128).astype(F32)
    for g in range(8):
        r_mat[:, g * 128 : (g + 1) * 128] = flat[pl.ds(g, 2 * n, stride=8), :].astype(BF16)

    update = dot(r_mat[...], m_mat[...])
    gain_p = gp_ref[...]
    for b in range(2):
        middle = pair[b].astype(F32) + update[:, b * 128 : (b + 1) * 128]
        unit, scale = layer_norm_parts(middle)
        normed = (unit * gain_p).astype(BF16)
        pn[b] = normed
        pre = dot(normed, ww[...])
        gate = jax.nn.sigmoid(pre)
        act_f = pre * gate
        act = act_f.astype(BF16)
        active[b] = act
        res_out[b] = (middle + dot(act, wn[...])).astype(BF16)
        dp = (d_act[b] * (gate + act_f * (1.0 - gate))).astype(BF16)
        d_pre[b] = dp
        d_normed = dot(dp, ww[...], 1, 1)
        grad = (cot[b].astype(F32) + layer_norm_adjoint(d_normed, gain_p, unit, scale)).astype(BF16)
        grad_rows[b] = grad
        g_mat[:, b * 128 : (b + 1) * 128] = grad

    for g in range(8):
        flat[pl.ds(g, 2 * n, stride=8), :] = dot(g_mat[...], m_mat[g * 128 : (g + 1) * 128, :], 1, 1)
    for zz in range(nz):
        for yy in range(ny):
            block = flat[(yy * nz + zz) * nx * 16 : (yy * nz + zz + 1) * nx * 16, :].astype(BF16)
            d_part[yy, slot_of(z, zz)] = block.reshape(nx, 16, 128)
    x_d_far.start()

    for block in range(8):
        dm = dot(r_mat[:, block * 128 : (block + 1) * 128], g_mat[...], 0, 0)
        for i in range(4):
            for b in range(2):
                dm_wide[b * 32 : (b + 1) * 32, (block * 4 + i) * 128 : (block * 4 + i + 1) * 128] = dm[
                    i * 32 : (i + 1) * 32, b * 128 : (b + 1) * 128
                ].astype(BF16)
    slab, height = w_part.shape[1] * w_part.shape[2], w_part.shape[2]

    def put(first, value):
        for i in range(0, value.shape[0], 16):
            peer, row = divmod(first + i, slab)
            w_part[peer, slot_of(z, row // height), row % height : row % height + 16] = value[i : i + 16].astype(BF16)

    for block in range(4):
        go = dot(left_t[...], dm_wide[:, block * 1024 : (block + 1) * 1024]) * (1.0 / 32.0)
        for i in range(8):
            put((block * 8 + i) * 32, go[:, i * 128 : (i + 1) * 128])
    put(1024, dot(active[0], cot[0], 0, 0) + dot(active[1], cot[1], 0, 0))
    up = dot(pn[0], d_pre[0], 0, 0) + dot(pn[1], d_pre[1], 0, 0)
    for i in range(4):
        put(1536 + i * 128, up[:, i * 128 : (i + 1) * 128])
    x_d_near.start()
    d_left_t = (dot(wide[...], dm_wide[...], 1, 1) * (1.0 / 32.0)).astype(BF16)

    def transposed(block):
        return jnp.concatenate(
            [
                jnp.concatenate([block[b * 8 : (b + 1) * 8, t * 32 : (t + 1) * 32] for t in range(4)], axis=0)
                for b in range(2)
            ],
            axis=1,
        ).astype(BF16)

    d_recv[p] = d_part[y, :, x]
    w_recv[p] = w_part[p]
    far_end = nz - 2 * half
    x_d_far.wait()
    d_mid[near:nz] = summed(d_recv, np_, near, nz).astype(BF16)
    x_d2.start(1, far_end)
    x_w1_far.start()
    x_d_near.wait()
    d_mid[0:near] = summed(d_recv, np_, 0, near).astype(BF16)
    x_d2.start(far_end)
    x_w1_near.start()
    d_recv2[z] = d_mid[half]
    x_w1_far.wait()
    w_mid[near:nz] = summed(w_recv, np_, near, nz).astype(BF16)
    x_w2.start(1, far_end)

    x_d2.wait()
    d_proj_t = jnp.concatenate([d_left_t, transposed(summed(d_recv2, nz))], axis=0)
    pwg = dot(d_proj_t, xn[...])
    pwg = jnp.concatenate([pwg[:, 0:128], pwg[:, 128:256]], axis=0).astype(BF16)
    p_part[...] = pwg.reshape(p_part.shape)
    x_p.start()

    x_w1_near.wait()
    w_mid[0:near] = summed(w_recv, np_, 0, near).astype(BF16)
    x_w2.start(far_end)
    w_recv2[z] = w_mid[half]

    p_recv[p] = p_part[p]
    d_norm = dot(d_proj_t, wp_ref[...], 0, 0)
    slope = layer_norm_adjoint(d_norm, gm_ref[...], unit_m[...], scale_m[:, 0:1])
    msa_grad_ref[...] = slope.astype(BF16)

    x_p.wait()
    total = summed(p_recv, np_).astype(BF16)
    p_mid[...] = total
    x_p2.start()
    p_recv2[z] = total

    for plan in (x_z, x_near, x_far, x_d_far, x_w1_far, x_d_near, x_w1_near):
        plan.done()

    x_w2.wait()
    total = summed(w_recv2, nz).astype(BF16)
    w_own[...] = total
    x_w3.start()
    w_all[p, half] = total

    x_w3.wait(nz - 2 * half)
    x_w_near.start()
    x_p2.wait()
    total = summed(p_recv2, nz).astype(BF16)
    p_own[...] = total
    x_p3.start()
    p_all[p] = total
    x_w3.wait(1, nz - 2 * half)
    x_w_far.start()
    for plan in (x_d2, x_p, x_w2, x_p2, x_w3):
        plan.done()
    x_p3.wait()
    proj_ref[...] = p_all[...].reshape(proj_ref.shape)
    x_w_near.wait()
    x_w_far.wait()
    for zz in range(nz):
        block = w_all[:, pl.ds(slot_of(z, zz), 1)]
        for pp in range(np_):
            weights_ref[pl.ds((pp * nz + zz) * height, height), :] = block[pp, 0]

    for plan in (x_p3, x_w_near, x_w_far):
        plan.done()


def final_kernel(
    pair_in, grad_in, msa_in, weights, proj,
    pair_out, grad_out_pair, msa_out, grad_out, proj_out, grad_up, grad_down,
    sem,
):
    copies = [
        pltpu.make_async_copy(pair_in, pair_out, sem.at[0]),
        pltpu.make_async_copy(grad_in, grad_out_pair, sem.at[1]),
    ]
    for copy in copies:
        copy.start()
    inv = 1.0 / 256.0
    for b in range(2):
        msa_out[:, b, :] = msa_in[b * 32 : (b + 1) * 32, :]
    for block in range(32):
        grad_out[pl.ds(factor_index(block), 32, stride=32), :] = (
            weights[block * 32 : (block + 1) * 32, :].astype(F32) * inv
        )
    grad_down[...] = weights[1024:1536, :].astype(F32) * inv
    for i in range(4):
        grad_up[:, i * 128 : (i + 1) * 128] = weights[1536 + i * 128 : 1536 + (i + 1) * 128, :].astype(F32) * inv
    for i in range(2):
        proj_out[:, i * 128 : (i + 1) * 128] = proj[i * 64 : (i + 1) * 64, :].astype(F32) * inv
    for copy in copies:
        copy.wait()


def local(dims, msa, pair, cot, gm, gp, wp, wc, ww, wn):
    ny, nz, nx = dims
    np_ = ny * nx
    n = np_ * nz
    wh = 2048 // n
    ph = 128 // np_
    hbm = pl.BlockSpec(memory_space=pltpu.HBM)
    vmem = pl.BlockSpec(memory_space=pltpu.VMEM)
    rows = pair.shape[1]

    def V(shape, dtype=BF16):
        return pltpu.VMEM(shape, dtype)

    D = pltpu.SemaphoreType.DMA
    scratch = [
        V((32, 2, 256)), V((1, 256), F32), V((1, 128), F32), V((64, 256)),
        V((2, rows, 128)), V((2, rows, 128)), V((1024, 128)), V((128, 512)), V((512, 128)),
        V((1024, 128), F32), V((32, 4096)), V((1024, 256)), V((2, rows, 512), F32), V((64, 256)),
        V((64, 256), F32), V((64, 128), F32), V((64, 32)), V((32, 64)),
        V((16, 128)), V((ny, nz, nx, 16, 128)), V((n * 16, 128), F32), V((rows, 1024)),
        V((2, rows, 128)), V((2, rows, 512)), V((2, rows, 512)), V((rows, 256)), V((64, 4096)),
        V((ny, nz, nx, 16, 128)), V((np_, nz, 16, 128)), V((nz, 16, 128)), V((nz, 16, 128)),
        V((np_, nz, wh, 128)), V((np_, nz, wh, 128)), V((nz, wh, 128)), V((nz, wh, 128)), V((wh, 128)),
        V((np_, nz, wh, 128)),
        V((np_, ph, 128)), V((np_, ph, 128)), V((ph, 128)), V((nz, ph, 128)), V((ph, 128)), V((np_, ph, 128)),
        D((9,)), D((5, nz)), D((5, nz)), D((10, np_)), D((10, np_)),
    ]
    outs = pl.pallas_call(
        functools.partial(main_kernel, dims),
        out_shape=[
            jax.ShapeDtypeStruct(pair.shape, BF16),
            jax.ShapeDtypeStruct(pair.shape, BF16),
            jax.ShapeDtypeStruct((64, 256), BF16),
            jax.ShapeDtypeStruct((2048, 128), BF16),
            jax.ShapeDtypeStruct((128, 128), BF16),
        ],
        in_specs=[hbm] * 9,
        out_specs=[vmem] * 5,
        scratch_shapes=scratch,
        compiler_params=pltpu.CompilerParams(
            collective_id=0, has_side_effects=True, vmem_limit_bytes=40 * 2**20
        ),
    )(*[
        pltpu.with_memory_space_constraint(v, pltpu.HBM)
        for v in (msa, pair, cot, gm.reshape(1, -1), gp.reshape(1, -1), wp.T, wc, ww, wn)
    ])
    results = pl.pallas_call(
        final_kernel,
        out_shape=[
            jax.ShapeDtypeStruct(pair.shape, BF16),
            jax.ShapeDtypeStruct(pair.shape, BF16),
            jax.ShapeDtypeStruct(msa.shape, BF16),
            jax.ShapeDtypeStruct((1024, 128), F32),
            jax.ShapeDtypeStruct((64, 256), F32),
            jax.ShapeDtypeStruct((128, 512), F32),
            jax.ShapeDtypeStruct((512, 128), F32),
        ],
        in_specs=[vmem] * 5,
        out_specs=[pl.BlockSpec(memory_space=pltpu.HBM)] * 2 + [vmem] * 5,
        scratch_shapes=[pltpu.SemaphoreType.DMA((2,))],
        compiler_params=pltpu.CompilerParams(vmem_limit_bytes=16 * 2**20),
    )(*outs)
    return tuple(r.T if i == 4 else r for i, r in enumerate(results))


DIMS = (2, 16, 4)


def solution(mesh, dims=DIMS):
    pairs = P(("cx", "res"), None, None)
    return jax.shard_map(
        functools.partial(local, dims),
        mesh=mesh,
        in_specs=(P("cx", "res", None), pairs, pairs, P(), P(), P(), P(), P(), P()),
        out_specs=(pairs, pairs, P("cx", "res", None), P("cx", None), P("cx", None), P("cx", None), P("cx", None)),
        check_vma=False,
    )
```

```python
import functools

import jax
import jax.numpy as jnp
from jax import lax
from jax.experimental import pallas as pl
from jax.experimental.pallas import tpu as pltpu
from jax.sharding import PartitionSpec as P

EPSILON = 1e-05
F32 = jnp.float32
BF16 = jnp.bfloat16
MESH = pl.DeviceIdType.MESH


def dot(a, b, ca=1, cb=0):
    return lax.dot_general(a, b, (((ca,), (cb,)), ((), ())), preferred_element_type=F32)


def layer_norm_parts(values):
    center = values - jnp.mean(values, axis=-1, keepdims=True)
    scale = lax.rsqrt(jnp.mean(center * center, axis=-1, keepdims=True) + EPSILON)
    return center * scale, scale


def layer_norm_adjoint(d_normed, gain, unit, scale):
    e = d_normed * gain
    return scale * (
        e
        - jnp.mean(e, axis=-1, keepdims=True)
        - unit * jnp.mean(e * unit, axis=-1, keepdims=True)
    )


def factor_index(block):
    return (block % 4) * 8 + block // 4


def main_kernel(
    dims,
    msa_hbm, pair_hbm, cot_hbm, gm_hbm, gp_hbm, wp_hbm, wc_hbm, ww_hbm, wn_hbm,
    res_out, grad_rows, msa_grad_ref, weights_ref, proj_ref,
    msa, gm_ref, gp_ref, wp_ref, pair, cot, wc, ww, wn,
    wcf, wide, m_mat, d_act, xn, unit_m, scale_m, left, left_t,
    own, gathered, flat, r_mat,
    pn, active, d_pre, g_mat, dm_wide,
    d_part, d_recv, d_mid, d_recv2,
    w_part, w_recv, w_mid, w_recv2, w_own, w_all,
    p_part, p_recv, p_mid, p_recv2, p_own, p_all,
    load_sem, z_send, z_recv, xy_send, xy_recv,
):
    ny, nz, nx = dims
    np_ = ny * nx
    n = np_ * nz
    half = nz // 4
    me = lax.axis_index("res")
    x = lax.rem(me, nx)
    z = lax.rem(me // nx, nz)
    y = me // (nx * nz)
    p = y * nx + x

    def at(yy, zz, xx):
        return {"res": (yy * nz + zz) * nx + xx}

    def z_device(zz):
        return at(y, zz, x)

    def xy_device(pp):
        return at(pp // nx, z, lax.rem(pp, nx))

    loads = [
        pltpu.make_async_copy(src, dst, load_sem.at[i])
        for i, (src, dst) in enumerate(
            [
                (msa_hbm, msa), (gm_hbm, gm_ref), (wp_hbm, wp_ref), (wc_hbm, wc), (cot_hbm, cot),
                (wn_hbm, wn), (ww_hbm, ww), (pair_hbm, pair), (gp_hbm, gp_ref),
            ]
        )
    ]
    def far_first(i):
        return lax.rem(z + nz // 2 + (1 - 2 * lax.rem(i, 2)) * ((i + 1) // 2), nz)

    barrier = pltpu.get_barrier_semaphore()

    @pl.loop(0, nz - 1, unroll=True)
    def _(i):
        pl.semaphore_signal(barrier, inc=1, device_id=z_device(far_first(i)), device_id_type=MESH)

    for load in loads[0:3]:
        load.start()

    @pl.loop(1, np_, unroll=True)
    def _(k):
        pl.semaphore_signal(barrier, inc=1, device_id=xy_device(lax.rem(p + k, np_)), device_id_type=MESH)

    for load in loads[3:]:
        load.start()

    class Exchange:
        def __init__(self, axis, stage, src, dst):
            self.stage, self.src, self.dst = stage, src, dst
            self.device, self.count, self.mine, self.send, self.recv, self.peer = {
                "z": (z_device, nz, z, z_send, z_recv, lambda i: far_first(i - 1)),
                "xy": (xy_device, np_, p, xy_send, xy_recv, lambda i: lax.rem(p + i, np_)),
            }[axis]

        def copy(self, to, slot, dst):
            return pltpu.make_async_remote_copy(
                src_ref=self.src(to), dst_ref=dst,
                send_sem=self.send.at[self.stage, to], recv_sem=self.recv.at[self.stage, slot],
                device_id=self.device(to), device_id_type=MESH)

        def start(self, first=1, last=None):
            @pl.loop(first, self.count if last is None else last, unroll=True)
            def _(i):
                to = self.peer(i)
                self.copy(to, self.mine, self.dst(to, self.mine)).start()

        def wait(self, first=1, last=None):
            @pl.loop(first, self.count if last is None else last, unroll=True)
            def _(i):
                slot = self.peer(i)
                self.copy(slot, slot, self.dst(self.mine, slot)).wait_recv()

        def done(self):
            @pl.loop(1, self.count, unroll=True)
            def _(i):
                to = self.peer(i)
                self.copy(to, to, self.dst(self.mine, to)).wait_send()

    def slot_of(at_z, from_z):
        return lax.rem(from_z - at_z + half + nz, nz)

    near = 2 * half + 1
    x_z = Exchange("z", 0, lambda to: own, lambda at_z, s: gathered.at[y, slot_of(at_z, s), x])
    x_near = Exchange(
        "xy", 0, lambda to: gathered.at[y, 0:near, x],
        lambda _, s: gathered.at[s // nx, 0:near, lax.rem(s, nx)])
    x_far = Exchange(
        "xy", 1, lambda to: gathered.at[y, near:nz, x],
        lambda _, s: gathered.at[s // nx, near:nz, lax.rem(s, nx)])
    x_d_far = Exchange(
        "xy", 2, lambda to: d_part.at[to // nx, near:nz, lax.rem(to, nx)], lambda _, s: d_recv.at[s, near:nz])
    x_d_near = Exchange(
        "xy", 8, lambda to: d_part.at[to // nx, 0:near, lax.rem(to, nx)], lambda _, s: d_recv.at[s, 0:near])
    x_d2 = Exchange("z", 1, lambda to: d_mid.at[slot_of(z, to)], lambda _, s: d_recv2.at[s])
    x_w1_far = Exchange("xy", 3, lambda to: w_part.at[to, near:nz], lambda _, s: w_recv.at[s, near:nz])
    x_w1_near = Exchange("xy", 9, lambda to: w_part.at[to, 0:near], lambda _, s: w_recv.at[s, 0:near])
    x_w2 = Exchange("z", 2, lambda to: w_mid.at[slot_of(z, to)], lambda _, s: w_recv2.at[s])
    x_w3 = Exchange("z", 3, lambda to: w_own, lambda at_z, s: w_all.at[p, slot_of(at_z, s)])
    x_w_near = Exchange("xy", 4, lambda to: w_all.at[p, 0:near], lambda _, s: w_all.at[s, 0:near])
    x_w_far = Exchange("xy", 5, lambda to: w_all.at[p, near:nz], lambda _, s: w_all.at[s, near:nz])
    x_p = Exchange("xy", 6, lambda to: p_part.at[to], lambda _, s: p_recv.at[s])
    x_p2 = Exchange("z", 4, lambda to: p_mid, lambda _, s: p_recv2.at[s])
    x_p3 = Exchange("xy", 7, lambda to: p_own, lambda _, s: p_all.at[s])

    def summed(ref, count, first=None, last=None):
        total = ref[0, first:last].astype(F32)
        for i in range(1, count):
            total += ref[i, first:last].astype(F32)
        return total

    for load in loads[0:3]:
        load.wait()
    rows = jnp.concatenate([msa[:, 0, :].astype(F32), msa[:, 1, :].astype(F32)], axis=0)
    unit, scale = layer_norm_parts(rows)
    unit_m[...] = unit
    scale_m[...] = jnp.broadcast_to(scale, scale_m.shape)
    normed = (unit * gm_ref[...]).astype(BF16)
    proj_t = dot(wp_ref[...], normed, 1, 1)
    right_t = proj_t[32:64]
    own_f = jnp.concatenate(
        [
            jnp.concatenate([right_t[t * 8 : (t + 1) * 8, b * 32 : (b + 1) * 32] for t in range(4)], axis=1)
            for b in range(2)
        ],
        axis=0,
    )
    own[...] = own_f.astype(BF16)
    xn[...] = normed
    pl.semaphore_wait(barrier, nz - 1 + np_ - 1)
    x_z.start()

    gathered[y, half, x] = own_f.astype(BF16)
    left_t[...] = proj_t[0:32].astype(BF16)
    left[...] = dot(normed, wp_ref[0:32, :], 1, 1).astype(BF16)
    loads[3].wait()
    wcf[...] = wc[...].astype(F32)
    for block in range(32):
        wide[:, block * 128 : (block + 1) * 128] = wcf[pl.ds(factor_index(block), 32, stride=32), :].astype(BF16)
    for block in range(32):
        part = dot(left[...], wide[:, block * 128 : (block + 1) * 128]) * (1.0 / 32.0)
        for b in range(2):
            m_mat[block * 32 : (block + 1) * 32, b * 128 : (b + 1) * 128] = part[b * 32 : (b + 1) * 32].astype(BF16)

    x_z.wait(nz - 2 * half)
    x_near.start()
    loads[4].wait()
    loads[5].wait()
    for b in range(2):
        d_act[b] = dot(cot[b], wn[...], 1, 1)
    for load in loads[6:9]:
        load.wait()
    x_z.wait(1, nz - 2 * half)
    x_far.start()

    x_near.wait()
    x_far.wait()
    for zz in range(nz):
        block = gathered[:, pl.ds(slot_of(z, zz), 1)]
        for yy in range(ny):
            flat[pl.ds((yy * nz + zz) * nx * 16, nx * 16), :] = block[yy].reshape(nx * 16, 128).astype(F32)
    for g in range(8):
        r_mat[:, g * 128 : (g + 1) * 128] = flat[pl.ds(g, 2 * n, stride=8), :].astype(BF16)

    update = dot(r_mat[...], m_mat[...])
    gain_p = gp_ref[...]
    for b in range(2):
        middle = pair[b].astype(F32) + update[:, b * 128 : (b + 1) * 128]
        unit, scale = layer_norm_parts(middle)
        normed = (unit * gain_p).astype(BF16)
        pn[b] = normed
        pre = dot(normed, ww[...])
        gate = jax.nn.sigmoid(pre)
        act_f = pre * gate
        act = act_f.astype(BF16)
        active[b] = act
        res_out[b] = (middle + dot(act, wn[...])).astype(BF16)
        dp = (d_act[b] * (gate + act_f * (1.0 - gate))).astype(BF16)
        d_pre[b] = dp
        d_normed = dot(dp, ww[...], 1, 1)
        grad = (cot[b].astype(F32) + layer_norm_adjoint(d_normed, gain_p, unit, scale)).astype(BF16)
        grad_rows[b] = grad
        g_mat[:, b * 128 : (b + 1) * 128] = grad

    for g in range(8):
        flat[pl.ds(g, 2 * n, stride=8), :] = dot(g_mat[...], m_mat[g * 128 : (g + 1) * 128, :], 1, 1)
    for zz in range(nz):
        for yy in range(ny):
            block = flat[(yy * nz + zz) * nx * 16 : (yy * nz + zz + 1) * nx * 16, :].astype(BF16)
            d_part[yy, slot_of(z, zz)] = block.reshape(nx, 16, 128)
    x_d_far.start()

    for block in range(8):
        dm = dot(r_mat[:, block * 128 : (block + 1) * 128], g_mat[...], 0, 0)
        for i in range(4):
            for b in range(2):
                dm_wide[b * 32 : (b + 1) * 32, (block * 4 + i) * 128 : (block * 4 + i + 1) * 128] = dm[
                    i * 32 : (i + 1) * 32, b * 128 : (b + 1) * 128
                ].astype(BF16)
    slab, height = w_part.shape[1] * w_part.shape[2], w_part.shape[2]

    def put(first, value):
        for i in range(0, value.shape[0], 16):
            peer, row = divmod(first + i, slab)
            w_part[peer, slot_of(z, row // height), row % height : row % height + 16] = value[i : i + 16].astype(BF16)

    for block in range(4):
        go = dot(left_t[...], dm_wide[:, block * 1024 : (block + 1) * 1024]) * (1.0 / 32.0)
        for i in range(8):
            put((block * 8 + i) * 32, go[:, i * 128 : (i + 1) * 128])
    put(1024, dot(active[0], cot[0], 0, 0) + dot(active[1], cot[1], 0, 0))
    up = dot(pn[0], d_pre[0], 0, 0) + dot(pn[1], d_pre[1], 0, 0)
    for i in range(4):
        put(1536 + i * 128, up[:, i * 128 : (i + 1) * 128])
    x_d_near.start()
    d_left_t = (dot(wide[...], dm_wide[...], 1, 1) * (1.0 / 32.0)).astype(BF16)

    def transposed(block):
        return jnp.concatenate(
            [
                jnp.concatenate([block[b * 8 : (b + 1) * 8, t * 32 : (t + 1) * 32] for t in range(4)], axis=0)
                for b in range(2)
            ],
            axis=1,
        ).astype(BF16)

    d_recv[p] = d_part[y, :, x]
    w_recv[p] = w_part[p]
    far_end = nz - 2 * half
    x_d_far.wait()
    d_mid[near:nz] = summed(d_recv, np_, near, nz).astype(BF16)
    x_d2.start(1, far_end)
    x_w1_far.start()
    x_d_near.wait()
    d_mid[0:near] = summed(d_recv, np_, 0, near).astype(BF16)
    x_d2.start(far_end)
    x_w1_near.start()
    d_recv2[z] = d_mid[half]
    x_w1_far.wait()
    w_mid[near:nz] = summed(w_recv, np_, near, nz).astype(BF16)
    x_w2.start(1, far_end)

    x_d2.wait()
    d_proj_t = jnp.concatenate([d_left_t, transposed(summed(d_recv2, nz))], axis=0)
    pwg = dot(d_proj_t, xn[...])
    pwg = jnp.concatenate([pwg[:, 0:128], pwg[:, 128:256]], axis=0).astype(BF16)
    p_part[...] = pwg.reshape(p_part.shape)
    x_p.start()

    x_w1_near.wait()
    w_mid[0:near] = summed(w_recv, np_, 0, near).astype(BF16)
    x_w2.start(far_end)
    w_recv2[z] = w_mid[half]

    p_recv[p] = p_part[p]
    d_norm = dot(d_proj_t, wp_ref[...], 0, 0)
    slope = layer_norm_adjoint(d_norm, gm_ref[...], unit_m[...], scale_m[:, 0:1])
    msa_grad_ref[...] = slope.astype(BF16)

    x_p.wait()
    total = summed(p_recv, np_).astype(BF16)
    p_mid[...] = total
    x_p2.start()
    p_recv2[z] = total

    x_w2.wait()
    total = summed(w_recv2, nz).astype(BF16)
    w_own[...] = total
    x_w3.start()
    w_all[p, half] = total
    for plan in (x_z, x_near, x_far, x_d_far, x_w1_far, x_d_near, x_w1_near):
        plan.done()

    x_w3.wait(nz - 2 * half)
    x_w_near.start()
    x_p2.wait()
    total = summed(p_recv2, nz).astype(BF16)
    p_own[...] = total
    x_p3.start()
    p_all[p] = total
    x_w3.wait(1, nz - 2 * half)
    x_w_far.start()
    for plan in (x_d2, x_p, x_w2, x_p2, x_w3):
        plan.done()
    x_p3.wait()
    proj_ref[...] = p_all[...].reshape(proj_ref.shape)
    x_w_near.wait()
    x_w_far.wait()
    for zz in range(nz):
        block = w_all[:, pl.ds(slot_of(z, zz), 1)]
        for pp in range(np_):
            weights_ref[pl.ds((pp * nz + zz) * height, height), :] = block[pp, 0]

    for plan in (x_p3, x_w_near, x_w_far):
        plan.done()


def final_kernel(
    pair_in, grad_in, msa_in, weights, proj,
    pair_out, grad_out_pair, msa_out, grad_out, proj_out, grad_up, grad_down,
    sem,
):
    copies = [
        pltpu.make_async_copy(pair_in, pair_out, sem.at[0]),
        pltpu.make_async_copy(grad_in, grad_out_pair, sem.at[1]),
    ]
    for copy in copies:
        copy.start()
    inv = 1.0 / 256.0
    for b in range(2):
        msa_out[:, b, :] = msa_in[b * 32 : (b + 1) * 32, :]
    for block in range(32):
        grad_out[pl.ds(factor_index(block), 32, stride=32), :] = (
            weights[block * 32 : (block + 1) * 32, :].astype(F32) * inv
        )
    grad_down[...] = weights[1024:1536, :].astype(F32) * inv
    for i in range(4):
        grad_up[:, i * 128 : (i + 1) * 128] = weights[1536 + i * 128 : 1536 + (i + 1) * 128, :].astype(F32) * inv
    for i in range(2):
        proj_out[:, i * 128 : (i + 1) * 128] = proj[i * 64 : (i + 1) * 64, :].astype(F32) * inv
    for copy in copies:
        copy.wait()


def local(dims, msa, pair, cot, gm, gp, wp, wc, ww, wn):
    ny, nz, nx = dims
    np_ = ny * nx
    n = np_ * nz
    wh = 2048 // n
    ph = 128 // np_
    hbm = pl.BlockSpec(memory_space=pltpu.HBM)
    vmem = pl.BlockSpec(memory_space=pltpu.VMEM)
    rows = pair.shape[1]

    def V(shape, dtype=BF16):
        return pltpu.VMEM(shape, dtype)

    D = pltpu.SemaphoreType.DMA
    scratch = [
        V((32, 2, 256)), V((1, 256), F32), V((1, 128), F32), V((64, 256)),
        V((2, rows, 128)), V((2, rows, 128)), V((1024, 128)), V((128, 512)), V((512, 128)),
        V((1024, 128), F32), V((32, 4096)), V((1024, 256)), V((2, rows, 512), F32), V((64, 256)),
        V((64, 256), F32), V((64, 128), F32), V((64, 32)), V((32, 64)),
        V((16, 128)), V((ny, nz, nx, 16, 128)), V((n * 16, 128), F32), V((rows, 1024)),
        V((2, rows, 128)), V((2, rows, 512)), V((2, rows, 512)), V((rows, 256)), V((64, 4096)),
        V((ny, nz, nx, 16, 128)), V((np_, nz, 16, 128)), V((nz, 16, 128)), V((nz, 16, 128)),
        V((np_, nz, wh, 128)), V((np_, nz, wh, 128)), V((nz, wh, 128)), V((nz, wh, 128)), V((wh, 128)),
        V((np_, nz, wh, 128)),
        V((np_, ph, 128)), V((np_, ph, 128)), V((ph, 128)), V((nz, ph, 128)), V((ph, 128)), V((np_, ph, 128)),
        D((9,)), D((5, nz)), D((5, nz)), D((10, np_)), D((10, np_)),
    ]
    outs = pl.pallas_call(
        functools.partial(main_kernel, dims),
        out_shape=[
            jax.ShapeDtypeStruct(pair.shape, BF16),
            jax.ShapeDtypeStruct(pair.shape, BF16),
            jax.ShapeDtypeStruct((64, 256), BF16),
            jax.ShapeDtypeStruct((2048, 128), BF16),
            jax.ShapeDtypeStruct((128, 128), BF16),
        ],
        in_specs=[hbm] * 9,
        out_specs=[vmem] * 5,
        scratch_shapes=scratch,
        compiler_params=pltpu.CompilerParams(
            collective_id=0, has_side_effects=True, vmem_limit_bytes=40 * 2**20
        ),
    )(*[
        pltpu.with_memory_space_constraint(v, pltpu.HBM)
        for v in (msa, pair, cot, gm.reshape(1, -1), gp.reshape(1, -1), wp.T, wc, ww, wn)
    ])
    results = pl.pallas_call(
        final_kernel,
        out_shape=[
            jax.ShapeDtypeStruct(pair.shape, BF16),
            jax.ShapeDtypeStruct(pair.shape, BF16),
            jax.ShapeDtypeStruct(msa.shape, BF16),
            jax.ShapeDtypeStruct((1024, 128), F32),
            jax.ShapeDtypeStruct((64, 256), F32),
            jax.ShapeDtypeStruct((128, 512), F32),
            jax.ShapeDtypeStruct((512, 128), F32),
        ],
        in_specs=[vmem] * 5,
        out_specs=[pl.BlockSpec(memory_space=pltpu.HBM)] * 2 + [vmem] * 5,
        scratch_shapes=[pltpu.SemaphoreType.DMA((2,))],
        compiler_params=pltpu.CompilerParams(vmem_limit_bytes=16 * 2**20),
    )(*outs)
    return tuple(r.T if i == 4 else r for i, r in enumerate(results))


DIMS = (2, 16, 4)


def solution(mesh, dims=DIMS):
    pairs = P(("cx", "res"), None, None)
    return jax.shard_map(
        functools.partial(local, dims),
        mesh=mesh,
        in_specs=(P("cx", "res", None), pairs, pairs, P(), P(), P(), P(), P(), P()),
        out_specs=(pairs, pairs, P("cx", "res", None), P("cx", None), P("cx", None), P("cx", None), P("cx", None)),
        check_vma=False,
    )
```

```python
import functools

import jax
import jax.numpy as jnp
from jax import lax
from jax.experimental import pallas as pl
from jax.experimental.pallas import tpu as pltpu
from jax.sharding import PartitionSpec as P

EPSILON = 1e-05
F32 = jnp.float32
BF16 = jnp.bfloat16
MESH = pl.DeviceIdType.MESH


def dot(a, b, ca=1, cb=0):
    return lax.dot_general(a, b, (((ca,), (cb,)), ((), ())), preferred_element_type=F32)


def layer_norm_parts(values):
    center = values - jnp.mean(values, axis=-1, keepdims=True)
    scale = lax.rsqrt(jnp.mean(center * center, axis=-1, keepdims=True) + EPSILON)
    return center * scale, scale


def layer_norm_adjoint(d_normed, gain, unit, scale):
    e = d_normed * gain
    return scale * (
        e
        - jnp.mean(e, axis=-1, keepdims=True)
        - unit * jnp.mean(e * unit, axis=-1, keepdims=True)
    )


def factor_index(block):
    return (block % 4) * 8 + block // 4


def main_kernel(
    dims,
    msa_hbm, pair_hbm, cot_hbm, gm_hbm, gp_hbm, wp_hbm, wc_hbm, ww_hbm, wn_hbm,
    res_out, grad_rows, msa_grad_ref, weights_ref, proj_ref,
    msa, gm_ref, gp_ref, wp_ref, pair, cot, wc, ww, wn,
    wcf, wide, m_mat, d_act, xn, unit_m, scale_m, left, left_t,
    own, gathered, flat, r_mat,
    pn, active, d_pre, g_mat, dm_wide,
    d_part, d_recv, d_mid, d_recv2,
    w_part, w_recv, w_mid, w_recv2, w_own, w_all,
    p_part, p_recv, p_mid, p_recv2, p_own, p_all,
    load_sem, z_send, z_recv, xy_send, xy_recv,
):
    ny, nz, nx = dims
    np_ = ny * nx
    n = np_ * nz
    half = nz // 4
    me = lax.axis_index("res")
    x = lax.rem(me, nx)
    z = lax.rem(me // nx, nz)
    y = me // (nx * nz)
    p = y * nx + x

    def at(yy, zz, xx):
        return {"res": (yy * nz + zz) * nx + xx}

    def z_device(zz):
        return at(y, zz, x)

    def xy_device(pp):
        return at(pp // nx, z, lax.rem(pp, nx))

    loads = [
        pltpu.make_async_copy(src, dst, load_sem.at[i])
        for i, (src, dst) in enumerate(
            [
                (msa_hbm, msa), (gm_hbm, gm_ref), (wp_hbm, wp_ref), (wc_hbm, wc), (cot_hbm, cot),
                (wn_hbm, wn), (ww_hbm, ww), (pair_hbm, pair), (gp_hbm, gp_ref),
            ]
        )
    ]
    def far_first(i):
        return lax.rem(z + nz // 2 + (1 - 2 * lax.rem(i, 2)) * ((i + 1) // 2), nz)

    barrier = pltpu.get_barrier_semaphore()

    @pl.loop(0, nz - 1, unroll=True)
    def _(i):
        pl.semaphore_signal(barrier, inc=1, device_id=z_device(far_first(i)), device_id_type=MESH)

    for load in loads[0:3]:
        load.start()

    @pl.loop(1, np_, unroll=True)
    def _(k):
        pl.semaphore_signal(barrier, inc=1, device_id=xy_device(lax.rem(p + k, np_)), device_id_type=MESH)

    for load in loads[3:]:
        load.start()

    class Exchange:
        def __init__(self, axis, stage, src, dst):
            self.stage, self.src, self.dst = stage, src, dst
            self.device, self.count, self.mine, self.send, self.recv, self.peer = {
                "z": (z_device, nz, z, z_send, z_recv, lambda i: far_first(i - 1)),
                "xy": (xy_device, np_, p, xy_send, xy_recv, lambda i: lax.rem(p + i, np_)),
            }[axis]

        def copy(self, to, slot, dst):
            return pltpu.make_async_remote_copy(
                src_ref=self.src(to), dst_ref=dst,
                send_sem=self.send.at[self.stage, to], recv_sem=self.recv.at[self.stage, slot],
                device_id=self.device(to), device_id_type=MESH)

        def start(self, first=1, last=None):
            @pl.loop(first, self.count if last is None else last, unroll=True)
            def _(i):
                to = self.peer(i)
                self.copy(to, self.mine, self.dst(to, self.mine)).start()

        def wait(self, first=1, last=None):
            @pl.loop(first, self.count if last is None else last, unroll=True)
            def _(i):
                slot = self.peer(i)
                self.copy(slot, slot, self.dst(self.mine, slot)).wait_recv()

        def done(self):
            @pl.loop(1, self.count, unroll=True)
            def _(i):
                to = self.peer(i)
                self.copy(to, to, self.dst(self.mine, to)).wait_send()

    def slot_of(at_z, from_z):
        return lax.rem(from_z - at_z + half + nz, nz)

    near = 2 * half + 1
    x_z = Exchange("z", 0, lambda to: own, lambda at_z, s: gathered.at[y, slot_of(at_z, s), x])
    x_near = Exchange(
        "xy", 0, lambda to: gathered.at[y, 0:near, x],
        lambda _, s: gathered.at[s // nx, 0:near, lax.rem(s, nx)])
    x_far = Exchange(
        "xy", 1, lambda to: gathered.at[y, near:nz, x],
        lambda _, s: gathered.at[s // nx, near:nz, lax.rem(s, nx)])
    x_d_far = Exchange(
        "xy", 2, lambda to: d_part.at[to // nx, near:nz, lax.rem(to, nx)], lambda _, s: d_recv.at[s, near:nz])
    x_d_near = Exchange(
        "xy", 8, lambda to: d_part.at[to // nx, 0:near, lax.rem(to, nx)], lambda _, s: d_recv.at[s, 0:near])
    x_d2 = Exchange("z", 1, lambda to: d_mid.at[slot_of(z, to)], lambda _, s: d_recv2.at[s])
    x_w1_far = Exchange("xy", 3, lambda to: w_part.at[to, near:nz], lambda _, s: w_recv.at[s, near:nz])
    x_w1_near = Exchange("xy", 9, lambda to: w_part.at[to, 0:near], lambda _, s: w_recv.at[s, 0:near])
    x_w2 = Exchange("z", 2, lambda to: w_mid.at[slot_of(z, to)], lambda _, s: w_recv2.at[s])
    x_w3 = Exchange("z", 3, lambda to: w_own, lambda at_z, s: w_all.at[p, slot_of(at_z, s)])
    x_w_near = Exchange("xy", 4, lambda to: w_all.at[p, 0:near], lambda _, s: w_all.at[s, 0:near])
    x_w_far = Exchange("xy", 5, lambda to: w_all.at[p, near:nz], lambda _, s: w_all.at[s, near:nz])
    x_p = Exchange("xy", 6, lambda to: p_part.at[to], lambda _, s: p_recv.at[s])
    x_p2 = Exchange("z", 4, lambda to: p_mid, lambda _, s: p_recv2.at[s])
    x_p3 = Exchange("xy", 7, lambda to: p_own, lambda _, s: p_all.at[s])

    def summed(ref, count, first=None, last=None):
        total = ref[0, first:last].astype(F32)
        for i in range(1, count):
            total += ref[i, first:last].astype(F32)
        return total

    for load in loads[0:3]:
        load.wait()
    rows = jnp.concatenate([msa[:, 0, :].astype(F32), msa[:, 1, :].astype(F32)], axis=0)
    unit, scale = layer_norm_parts(rows)
    unit_m[...] = unit
    scale_m[...] = jnp.broadcast_to(scale, scale_m.shape)
    normed = (unit * gm_ref[...]).astype(BF16)
    proj_t = dot(wp_ref[...], normed, 1, 1)
    right_t = proj_t[32:64]
    own_f = jnp.concatenate(
        [
            jnp.concatenate([right_t[t * 8 : (t + 1) * 8, b * 32 : (b + 1) * 32] for t in range(4)], axis=1)
            for b in range(2)
        ],
        axis=0,
    )
    own[...] = own_f.astype(BF16)
    xn[...] = normed
    pl.semaphore_wait(barrier, nz - 1 + np_ - 1)
    x_z.start()

    gathered[y, half, x] = own_f.astype(BF16)
    left_t[...] = proj_t[0:32].astype(BF16)
    left[...] = dot(normed, wp_ref[0:32, :], 1, 1).astype(BF16)
    loads[3].wait()
    wcf[...] = wc[...].astype(F32)
    for block in range(32):
        wide[:, block * 128 : (block + 1) * 128] = wcf[pl.ds(factor_index(block), 32, stride=32), :].astype(BF16)
    for block in range(32):
        part = dot(left[...], wide[:, block * 128 : (block + 1) * 128]) * (1.0 / 32.0)
        for b in range(2):
            m_mat[block * 32 : (block + 1) * 32, b * 128 : (b + 1) * 128] = part[b * 32 : (b + 1) * 32].astype(BF16)

    x_z.wait(nz - 2 * half)
    x_near.start()
    loads[4].wait()
    loads[5].wait()
    for b in range(2):
        d_act[b] = dot(cot[b], wn[...], 1, 1)
    for load in loads[6:9]:
        load.wait()
    x_z.wait(1, nz - 2 * half)
    x_far.start()

    x_near.wait()
    x_far.wait()
    for zz in range(nz):
        block = gathered[:, pl.ds(slot_of(z, zz), 1)]
        for yy in range(ny):
            flat[pl.ds((yy * nz + zz) * nx * 16, nx * 16), :] = block[yy].reshape(nx * 16, 128).astype(F32)
    for g in range(8):
        r_mat[:, g * 128 : (g + 1) * 128] = flat[pl.ds(g, 2 * n, stride=8), :].astype(BF16)

    update = dot(r_mat[...], m_mat[...])
    gain_p = gp_ref[...]
    for b in range(2):
        middle = pair[b].astype(F32) + update[:, b * 128 : (b + 1) * 128]
        unit, scale = layer_norm_parts(middle)
        normed = (unit * gain_p).astype(BF16)
        pn[b] = normed
        pre = dot(normed, ww[...])
        gate = jax.nn.sigmoid(pre)
        act_f = pre * gate
        act = act_f.astype(BF16)
        active[b] = act
        res_out[b] = (middle + dot(act, wn[...])).astype(BF16)
        dp = (d_act[b] * (gate + act_f * (1.0 - gate))).astype(BF16)
        d_pre[b] = dp
        d_normed = dot(dp, ww[...], 1, 1)
        grad = (cot[b].astype(F32) + layer_norm_adjoint(d_normed, gain_p, unit, scale)).astype(BF16)
        grad_rows[b] = grad
        g_mat[:, b * 128 : (b + 1) * 128] = grad

    for g in range(8):
        flat[pl.ds(g, 2 * n, stride=8), :] = dot(g_mat[...], m_mat[g * 128 : (g + 1) * 128, :], 1, 1)
    for zz in range(nz):
        for yy in range(ny):
            block = flat[(yy * nz + zz) * nx * 16 : (yy * nz + zz + 1) * nx * 16, :].astype(BF16)
            d_part[yy, slot_of(z, zz)] = block.reshape(nx, 16, 128)
    x_d_far.start()
    x_d_near.start()

    for block in range(8):
        dm = dot(r_mat[:, block * 128 : (block + 1) * 128], g_mat[...], 0, 0)
        for i in range(4):
            for b in range(2):
                dm_wide[b * 32 : (b + 1) * 32, (block * 4 + i) * 128 : (block * 4 + i + 1) * 128] = dm[
                    i * 32 : (i + 1) * 32, b * 128 : (b + 1) * 128
                ].astype(BF16)
    slab, height = w_part.shape[1] * w_part.shape[2], w_part.shape[2]

    def put(first, value):
        for i in range(0, value.shape[0], 16):
            peer, row = divmod(first + i, slab)
            w_part[peer, slot_of(z, row // height), row % height : row % height + 16] = value[i : i + 16].astype(BF16)

    for block in range(4):
        go = dot(left_t[...], dm_wide[:, block * 1024 : (block + 1) * 1024]) * (1.0 / 32.0)
        for i in range(8):
            put((block * 8 + i) * 32, go[:, i * 128 : (i + 1) * 128])
    put(1024, dot(active[0], cot[0], 0, 0) + dot(active[1], cot[1], 0, 0))
    up = dot(pn[0], d_pre[0], 0, 0) + dot(pn[1], d_pre[1], 0, 0)
    for i in range(4):
        put(1536 + i * 128, up[:, i * 128 : (i + 1) * 128])
    d_left_t = (dot(wide[...], dm_wide[...], 1, 1) * (1.0 / 32.0)).astype(BF16)

    def transposed(block):
        return jnp.concatenate(
            [
                jnp.concatenate([block[b * 8 : (b + 1) * 8, t * 32 : (t + 1) * 32] for t in range(4)], axis=0)
                for b in range(2)
            ],
            axis=1,
        ).astype(BF16)

    d_recv[p] = d_part[y, :, x]
    w_recv[p] = w_part[p]
    far_end = nz - 2 * half
    x_d_far.wait()
    d_mid[near:nz] = summed(d_recv, np_, near, nz).astype(BF16)
    x_d2.start(1, far_end)
    x_w1_far.start()
    x_d_near.wait()
    d_mid[0:near] = summed(d_recv, np_, 0, near).astype(BF16)
    x_d2.start(far_end)
    x_w1_near.start()
    d_recv2[z] = d_mid[half]
    x_w1_far.wait()
    w_mid[near:nz] = summed(w_recv, np_, near, nz).astype(BF16)
    x_w2.start(1, far_end)

    x_d2.wait()
    d_proj_t = jnp.concatenate([d_left_t, transposed(summed(d_recv2, nz))], axis=0)
    pwg = dot(d_proj_t, xn[...])
    pwg = jnp.concatenate([pwg[:, 0:128], pwg[:, 128:256]], axis=0).astype(BF16)
    p_part[...] = pwg.reshape(p_part.shape)
    x_p.start()

    x_w1_near.wait()
    w_mid[0:near] = summed(w_recv, np_, 0, near).astype(BF16)
    x_w2.start(far_end)
    w_recv2[z] = w_mid[half]

    p_recv[p] = p_part[p]
    d_norm = dot(d_proj_t, wp_ref[...], 0, 0)
    slope = layer_norm_adjoint(d_norm, gm_ref[...], unit_m[...], scale_m[:, 0:1])
    msa_grad_ref[...] = slope.astype(BF16)

    x_p.wait()
    total = summed(p_recv, np_).astype(BF16)
    p_mid[...] = total
    x_p2.start()
    p_recv2[z] = total

    for plan in (x_z, x_near, x_far, x_d_far, x_w1_far, x_d_near, x_w1_near):
        plan.done()

    x_w2.wait()
    total = summed(w_recv2, nz).astype(BF16)
    w_own[...] = total
    x_w3.start()
    w_all[p, half] = total

    x_w3.wait(nz - 2 * half)
    x_w_near.start()
    x_p2.wait()
    total = summed(p_recv2, nz).astype(BF16)
    p_own[...] = total
    x_p3.start()
    p_all[p] = total
    x_w3.wait(1, nz - 2 * half)
    x_w_far.start()
    for plan in (x_d2, x_p, x_w2, x_p2, x_w3):
        plan.done()
    x_p3.wait()
    proj_ref[...] = p_all[...].reshape(proj_ref.shape)
    x_w_near.wait()
    x_w_far.wait()
    for zz in range(nz):
        block = w_all[:, pl.ds(slot_of(z, zz), 1)]
        for pp in range(np_):
            weights_ref[pl.ds((pp * nz + zz) * height, height), :] = block[pp, 0]

    for plan in (x_p3, x_w_near, x_w_far):
        plan.done()


def final_kernel(
    pair_in, grad_in, msa_in, weights, proj,
    pair_out, grad_out_pair, msa_out, grad_out, proj_out, grad_up, grad_down,
    sem,
):
    copies = [
        pltpu.make_async_copy(pair_in, pair_out, sem.at[0]),
        pltpu.make_async_copy(grad_in, grad_out_pair, sem.at[1]),
    ]
    for copy in copies:
        copy.start()
    inv = 1.0 / 256.0
    for b in range(2):
        msa_out[:, b, :] = msa_in[b * 32 : (b + 1) * 32, :]
    for block in range(32):
        grad_out[pl.ds(factor_index(block), 32, stride=32), :] = (
            weights[block * 32 : (block + 1) * 32, :].astype(F32) * inv
        )
    grad_down[...] = weights[1024:1536, :].astype(F32) * inv
    for i in range(4):
        grad_up[:, i * 128 : (i + 1) * 128] = weights[1536 + i * 128 : 1536 + (i + 1) * 128, :].astype(F32) * inv
    for i in range(2):
        proj_out[:, i * 128 : (i + 1) * 128] = proj[i * 64 : (i + 1) * 64, :].astype(F32) * inv
    for copy in copies:
        copy.wait()


def local(dims, msa, pair, cot, gm, gp, wp, wc, ww, wn):
    ny, nz, nx = dims
    np_ = ny * nx
    n = np_ * nz
    wh = 2048 // n
    ph = 128 // np_
    hbm = pl.BlockSpec(memory_space=pltpu.HBM)
    vmem = pl.BlockSpec(memory_space=pltpu.VMEM)
    rows = pair.shape[1]

    def V(shape, dtype=BF16):
        return pltpu.VMEM(shape, dtype)

    D = pltpu.SemaphoreType.DMA
    scratch = [
        V((32, 2, 256)), V((1, 256), F32), V((1, 128), F32), V((64, 256)),
        V((2, rows, 128)), V((2, rows, 128)), V((1024, 128)), V((128, 512)), V((512, 128)),
        V((1024, 128), F32), V((32, 4096)), V((1024, 256)), V((2, rows, 512), F32), V((64, 256)),
        V((64, 256), F32), V((64, 128), F32), V((64, 32)), V((32, 64)),
        V((16, 128)), V((ny, nz, nx, 16, 128)), V((n * 16, 128), F32), V((rows, 1024)),
        V((2, rows, 128)), V((2, rows, 512)), V((2, rows, 512)), V((rows, 256)), V((64, 4096)),
        V((ny, nz, nx, 16, 128)), V((np_, nz, 16, 128)), V((nz, 16, 128)), V((nz, 16, 128)),
        V((np_, nz, wh, 128)), V((np_, nz, wh, 128)), V((nz, wh, 128)), V((nz, wh, 128)), V((wh, 128)),
        V((np_, nz, wh, 128)),
        V((np_, ph, 128)), V((np_, ph, 128)), V((ph, 128)), V((nz, ph, 128)), V((ph, 128)), V((np_, ph, 128)),
        D((9,)), D((5, nz)), D((5, nz)), D((10, np_)), D((10, np_)),
    ]
    outs = pl.pallas_call(
        functools.partial(main_kernel, dims),
        out_shape=[
            jax.ShapeDtypeStruct(pair.shape, BF16),
            jax.ShapeDtypeStruct(pair.shape, BF16),
            jax.ShapeDtypeStruct((64, 256), BF16),
            jax.ShapeDtypeStruct((2048, 128), BF16),
            jax.ShapeDtypeStruct((128, 128), BF16),
        ],
        in_specs=[hbm] * 9,
        out_specs=[vmem] * 5,
        scratch_shapes=scratch,
        compiler_params=pltpu.CompilerParams(
            collective_id=0, has_side_effects=True, vmem_limit_bytes=40 * 2**20
        ),
    )(*[
        pltpu.with_memory_space_constraint(v, pltpu.HBM)
        for v in (msa, pair, cot, gm.reshape(1, -1), gp.reshape(1, -1), wp.T, wc, ww, wn)
    ])
    results = pl.pallas_call(
        final_kernel,
        out_shape=[
            jax.ShapeDtypeStruct(pair.shape, BF16),
            jax.ShapeDtypeStruct(pair.shape, BF16),
            jax.ShapeDtypeStruct(msa.shape, BF16),
            jax.ShapeDtypeStruct((1024, 128), F32),
            jax.ShapeDtypeStruct((64, 256), F32),
            jax.ShapeDtypeStruct((128, 512), F32),
            jax.ShapeDtypeStruct((512, 128), F32),
        ],
        in_specs=[vmem] * 5,
        out_specs=[pl.BlockSpec(memory_space=pltpu.HBM)] * 2 + [vmem] * 5,
        scratch_shapes=[pltpu.SemaphoreType.DMA((2,))],
        compiler_params=pltpu.CompilerParams(vmem_limit_bytes=16 * 2**20),
    )(*outs)
    return tuple(r.T if i == 4 else r for i, r in enumerate(results))


DIMS = (2, 16, 4)


def solution(mesh, dims=DIMS):
    pairs = P(("cx", "res"), None, None)
    return jax.shard_map(
        functools.partial(local, dims),
        mesh=mesh,
        in_specs=(P("cx", "res", None), pairs, pairs, P(), P(), P(), P(), P(), P()),
        out_specs=(pairs, pairs, P("cx", "res", None), P("cx", None), P("cx", None), P("cx", None), P("cx", None)),
        check_vma=False,
    )
```
